128 devices in a mesh: ctx: 16 (over z, x), tensor: 8 (over y, core).
Axes of the slice: x: 4, y: 4, z: 4, core: 2. Of those that a mesh axis runs over, the one named last changes fastest.
Arguments:
- hidden: bfloat16 [2048, 8192], P('ctx', 'tensor'), may hold values from -6 to 6
- norm_gain: float32 [8192], replicated, may hold values from 0.1 to 1.9
- w_query: bfloat16 [8192, 8192], P(None, 'tensor'), may hold values from -0.0625 to 0.0625
- w_key: bfloat16 [8192, 1024], P(None, 'tensor'), may hold values from -0.0625 to 0.0625
- w_value: bfloat16 [8192, 1024], P(None, 'tensor'), may hold values from -0.0625 to 0.0625
- cache_keys: bfloat16 [16384, 1024], P('ctx', 'tensor'), may hold values from -600 to 600
- cache_values: bfloat16 [16384, 1024], P('ctx', 'tensor'), may hold values from -6 to 6
- cache_lengths: int32 [16], P('ctx'), may hold values from 1 to 1024, 12288 in all
Outputs:
- attention: bfloat16 [2048, 8192], P('ctx', 'tensor')
The draws below stay inside these ranges and needn't reach their ends.
Inputs may be any that keep to these rules, and one draw needn't show every extreme that they name: `cache_lengths`: each shard's valid slots form a prefix of its cache; some shard is full.
All inputs are finite; a program needn't handle non-finite values.
Results may differ from the reference program's by a relative error of at most 0.02.
The reference program's roundings to bfloat16 on the way count: a program that leaves them out, or rounds other values in their place, can miss the bound.
Values may be sent and summed in bfloat16 or wider, within the bound.
A program may use at most 128 MiB of HBM per device.

```python
import math
import jax
import jax.numpy as jnp
import numpy as np
from jax import lax

D = 8192
HEADS = 64
KV_HEADS = 8
HEAD_DIM = 128
Q_DEV = 128
CTX_DEV = 1024
SHARDS = 16
QB = 2048
CONTEXT = 16384


def draw_cache_keys(key, part):
    key = jax.random.fold_in(key, 7)
    rows = SHARDS * CTX_DEV
    width = KV_HEADS * HEAD_DIM
    key_a = jax.random.fold_in(key, 0)
    result = 2.0 * jax.random.normal(key_a, (rows, width), jnp.float32)
    return jnp.clip(result, -600.0, 600.0).astype(jnp.bfloat16)


def shard_levels(stream_key, dims, pieces, low, high):
    factor_of, own = 1.0, jax.random.fold_in(stream_key, 6)
    for position, shards_of in pieces:
        draws = jnp.exp(jax.random.uniform(jax.random.fold_in(own, position), (shards_of,), jnp.float32, low / len(pieces), high / len(pieces)))
        factor_of = factor_of * jnp.repeat(draws, dims[position] // shards_of).reshape([-1 if axis == position else 1 for axis in range(len(dims))])
    return factor_of


def length_profile(amount, total, most, lean):
    portions = [(1 << 20) // math.isqrt(rank ** lean) + 1 for rank in range(2, amount + 1)]
    spare, counts = total - most - (amount - 1), [1] * (amount - 1)
    while spare > 0:
        movable = [i for i in range(amount - 1) if counts[i] < most]
        mass, remaining = sum([portions[i] for i in movable]), spare
        for i in movable:
            more = min(most - counts[i], max(1, remaining * portions[i] // mass), spare)
            counts[i] = counts[i] + more
            spare = spare - more
    return np.array([most] + counts)


def uneven(key, amount, total, reach, skew):
    if amount == 2:
        one = jax.random.randint(key, (), max(1, total - reach), min(reach, total - 1) + 1)
        return jnp.stack([one, total - one])
    sizes = jnp.asarray(length_profile(amount, total, reach, skew), jnp.int32)
    twos = (amount - 1) // 2
    donor, taker = sizes[1:1 + 2 * twos:2], sizes[2:2 + 2 * twos:2]
    margin = jnp.minimum(donor - 1, reach - taker)
    moved = jax.random.randint(jax.random.fold_in(key, 1), (twos,), 0, 1 << 20) % (margin + 1)
    sizes = sizes.at[1:1 + 2 * twos:2].set(donor - moved).at[2:2 + 2 * twos:2].set(taker + moved)
    return sizes[jax.random.permutation(jax.random.fold_in(key, 2), amount)]


def gaussian(own_key, shape, scale, reach, shards=(), kind=jnp.bfloat16):
    values = jax.random.normal(own_key, shape, jnp.float32) * scale
    if len(shards) > 0:
        values = shard_levels(own_key, shape, shards, -0.22, 0.18) * values
    return jnp.clip(values, min=-reach, max=reach).astype(kind)


def setup_inputs(seed: int = 0) -> dict:
    splits = jax.random.split(jax.random.key(seed), 9)
    hidden = gaussian(splits[0], (QB, D), 1.0, 6.0, ((0, 16), (1, 8)))
    norm_gain = jnp.clip(1.0 + 0.18 * jax.random.normal(splits[1], (D,), jnp.float32), 0.1, 1.9)
    w_query = gaussian(splits[2], (D, HEADS * HEAD_DIM), D ** -0.5, 0.0625, ((1, 8),))
    w_key = gaussian(splits[3], (D, KV_HEADS * HEAD_DIM), D ** -0.5, 0.0625, ((1, 8),))
    w_value = gaussian(splits[4], (D, KV_HEADS * HEAD_DIM), D ** -0.5, 0.0625, ((1, 8),))
    cache_keys = draw_cache_keys(jax.random.fold_in(splits[8], 71), 0)
    cache_values = gaussian(splits[6], (CONTEXT, KV_HEADS * HEAD_DIM), 1.0, 6.0, ((0, 16), (1, 8)))
    cache_lengths = uneven(splits[7], SHARDS, SHARDS * CTX_DEV * 3 // 4, CTX_DEV, 1).astype(jnp.int32)
    return {"hidden": hidden, "norm_gain": norm_gain, "w_query": w_query, "w_key": w_key, "w_value": w_value, "cache_keys": cache_keys, "cache_values": cache_values, "cache_lengths": cache_lengths}


def rotate(values, positions, head_dim):
    rows = values.shape[0]
    heads = values.shape[1] // head_dim
    shaped = values.reshape(rows, heads, head_dim)
    half = head_dim // 2
    freq = jnp.power(jnp.float32(500000.0), -(jnp.arange(half, dtype=jnp.float32) * 2.0 / head_dim))
    angle = positions.astype(jnp.float32)[:, None] * freq[None, :]
    cosine = jnp.cos(angle)[:, None, :]
    sine = jnp.sin(angle)[:, None, :]
    first = shaped[:, :, :half]
    second = shaped[:, :, half:]
    turned = jnp.concatenate([first * cosine - second * sine, second * cosine + first * sine], axis=2)
    return turned.reshape(rows, heads * head_dim)

def attend(queries, keys, values, valid_len, own_start, ctx_len, head_dim, kv_heads):
    total = queries.shape[0]
    width = queries.shape[1]
    heads = width // head_dim
    group = heads // kv_heads
    block = 512 if total % 512 == 0 else total
    count = total // block
    slots = keys.shape[0]
    key_heads = keys.reshape(slots, kv_heads, head_dim)
    value_heads = values.reshape(slots, kv_heads, head_dim)
    slot_ids = jnp.arange(slots, dtype=jnp.int32)
    scale = 1.0 / head_dim ** 0.5

    def one_block(index):
        begin = (index * block).astype(jnp.int32)
        rows_q = lax.dynamic_slice_in_dim(queries, begin, block, 0).reshape(block, kv_heads, group, head_dim)
        score = jnp.einsum('bkgd,tkd->bkgt', rows_q, key_heads, preferred_element_type=jnp.float32) * scale
        row_ids = begin + jnp.arange(block, dtype=jnp.int32)
        cached = (slot_ids < ctx_len) & (slot_ids < valid_len)
        own = (slot_ids >= ctx_len)[None, :] & ((own_start + slot_ids - ctx_len)[None, :] <= row_ids[:, None])
        valid = cached[None, :] | own
        score = jnp.where(valid[:, None, None, :], score, jnp.float32(-1e+30))
        top = lax.optimization_barrier(jnp.max(score, axis=3, keepdims=True))
        prob = jnp.where(valid[:, None, None, :], jnp.exp(score - top), jnp.float32(0.0))
        total_p = lax.optimization_barrier(jnp.sum(prob, axis=3))
        prob_low = prob.astype(jnp.bfloat16)
        out = jnp.einsum('bkgt,tkd->bkgd', prob_low, value_heads, preferred_element_type=jnp.float32)
        part = (out / total_p[..., None]).astype(jnp.bfloat16).reshape(block, width)
        lse = (top[..., 0] + jnp.log(total_p)).reshape(block, heads)
        return (part, lse)
    parts, lses = lax.map(one_block, jnp.arange(count, dtype=jnp.int32))
    return (parts.reshape(total, width), lses.reshape(total, heads))

def reference(hidden, norm_gain, w_query, w_key, w_value, cache_keys, cache_values, cache_lengths):
    head_dim = HEAD_DIM
    wide = hidden.astype(jnp.float32)
    normed = (wide * lax.rsqrt(lax.optimization_barrier(jnp.mean(wide * wide, axis=1, keepdims=True)) + 1e-05) * norm_gain[None, :]).astype(jnp.bfloat16)
    positions = SHARDS * CTX_DEV + jnp.arange(QB, dtype=jnp.int32)
    query = rotate(jnp.dot(normed, w_query, preferred_element_type=jnp.float32), positions, head_dim).astype(jnp.bfloat16)
    own_keys = rotate(jnp.dot(normed, w_key, preferred_element_type=jnp.float32), positions, head_dim).astype(jnp.bfloat16)
    own_values = jnp.dot(normed, w_value, preferred_element_type=jnp.float32).astype(jnp.bfloat16)
    kv_width = KV_HEADS * HEAD_DIM
    shard_keys = cache_keys.reshape(SHARDS, CTX_DEV, kv_width)
    shard_values = cache_values.reshape(SHARDS, CTX_DEV, kv_width)
    block_keys = own_keys.reshape(SHARDS, Q_DEV, kv_width)
    block_values = own_values.reshape(SHARDS, Q_DEV, kv_width)

    def step(carry, group_index):
        best, numer, denom = carry
        keys = jnp.concatenate([shard_keys[group_index], block_keys[group_index]], axis=0)
        values = jnp.concatenate([shard_values[group_index], block_values[group_index]], axis=0)
        part, lse = attend(query, keys, values, cache_lengths[group_index], group_index * Q_DEV, CTX_DEV, HEAD_DIM, KV_HEADS)
        fresh = jnp.maximum(best, lse)
        old_w = jnp.exp(best - fresh)
        new_w = jnp.exp(lse - fresh)
        shaped = part.astype(jnp.float32).reshape(QB, HEADS, HEAD_DIM)
        numer = numer * old_w[..., None] + new_w[..., None] * shaped
        denom = denom * old_w + new_w
        return ((fresh, numer, denom), None)
    start = (jnp.full((QB, HEADS), -1e+30, jnp.float32), jnp.zeros((QB, HEADS, HEAD_DIM), jnp.float32), jnp.zeros((QB, HEADS), jnp.float32))
    (best, numer, denom), unused = lax.scan(step, start, jnp.arange(SHARDS, dtype=jnp.int32))
    return (numer / denom[..., None]).reshape(QB, HEADS * HEAD_DIM).astype(jnp.bfloat16)
```

```python
import functools

import jax
import jax.numpy as jnp
import numpy as np
from jax import lax
from jax.experimental import pallas as pl
from jax.experimental.pallas import tpu as pltpu
from jax.sharding import PartitionSpec as P

HEAD_DIM = 128
ROWS = 128
FEAT = 1024
SLOTS = 1024
HEADS = 8
HALF = 4 * ROWS
TILE = 512
KEYS = 4 * SLOTS + 4 * ROWS
WIDTH = HEADS * HEAD_DIM + 2 * HEAD_DIM
SCALE = 1.0 / HEAD_DIM**0.5
EXP2 = SCALE / float(np.log(2.0))
LOW = -1e30
MESH = pl.DeviceIdType.MESH
NT = (((1,), (1,)), ((), ()))
F32, BF16 = jnp.float32, jnp.bfloat16


def rotary_tables():
    half = HEAD_DIM // 2
    freq = 500000.0 ** (-2.0 * np.arange(half) / HEAD_DIM)
    angle = (16384 + np.arange(2048))[:, None] * freq[None, :]
    cosine, sine = np.cos(angle), np.sin(angle)
    both = np.stack(
        [np.concatenate([cosine, cosine], 1), np.concatenate([-sine, sine], 1)]
    )
    both = both.reshape(2, 16, ROWS, HEAD_DIM).transpose(1, 0, 2, 3)
    return both.astype(np.float32)


def eye():
    row = lax.broadcasted_iota(jnp.int32, (ROWS, ROWS), 0)
    col = lax.broadcasted_iota(jnp.int32, (ROWS, ROWS), 1)
    return row == col


def to_row(column):
    return jnp.sum(jnp.where(eye(), column, 0.0), axis=0, keepdims=True)


def to_column(row):
    wide = jnp.broadcast_to(row, (ROWS, ROWS))
    return jnp.sum(jnp.where(eye(), wide, 0.0), axis=1, keepdims=True)


def tile_step(q, state, keys, values, bias=None):
    s = lax.dot_general(q, keys, NT, preferred_element_type=F32)
    if bias is not None:
        s = (s.reshape(4, ROWS, TILE) + bias[None]).reshape(HALF, TILE)
    top = jnp.max(s, axis=1, keepdims=True)
    if state is not None:
        top = jnp.maximum(state[0], top)
    p = jnp.exp2((s - top) * EXP2).astype(BF16)
    add = jnp.dot(p, values, preferred_element_type=F32)
    if state is None:
        return top, add
    return top, state[1] * jnp.exp2((state[0] - top) * EXP2) + add


def kernel(
    hid, gain, wq, wk, wv, ck, cv, lens, tab, out,
    w, hbuf, gbuf, tabv, ssq, rs, acc, kvraw, lensb, kp, vp, qbuf, pout, pin, lout, lin,
    wsem, lsem, hs, hr, ss, sr, ks, kr, ls, lr, os_, or_, qs, qr, ps, pr, es, er,
):
    ci, ti = lax.axis_index("ctx"), lax.axis_index("tensor")
    z, x = lax.div(ci, 4), lax.rem(ci, 4)
    y, c = lax.div(ti, 2), lax.rem(ti, 2)

    def at_y(d, other=False):
        core = 1 - c if other else c
        return 2 * lax.rem(y + d, 4) + core

    def at_x(d):
        return lax.rem(x + d, 4)

    def at_z(d):
        return lax.rem(z + d, 4)

    def x_dev(d):
        return (4 * z + at_x(d), ti)

    def z_dev(d):
        return (4 * at_z(d) + x, ti)

    def y_dev(d):
        return (ci, at_y(d))

    sib = (ci, at_y(0, True))
    sends = []

    def remote(src, dst, send_sem, recv_sem, device):
        return pltpu.make_async_remote_copy(
            src_ref=src, dst_ref=dst, send_sem=send_sem, recv_sem=recv_sem,
            device_id=device, device_id_type=MESH,
        )

    def send(*args):
        copy = remote(*args)
        copy.start()
        sends.append(copy)

    order = [at_y(0), at_y(0, True), at_y(3), at_y(1), at_y(3, True), at_y(1, True), at_y(2), at_y(2, True)]
    own_h = pltpu.make_async_copy(hid, hbuf.at[ti], lsem.at[0])
    own_h.start()
    load_gain = pltpu.make_async_copy(gain, gbuf, lsem.at[1])
    load_gain.start()

    barrier = pltpu.get_barrier_semaphore()
    peers = [(ci, lax.rem(ti + d, 8)) for d in range(1, 8)]
    peers += [x_dev(d) for d in (1, 2, 3)] + [z_dev(d) for d in (1, 2, 3)]
    for peer in peers:
        pl.semaphore_signal(barrier, inc=1, device_id=peer, device_id_type=MESH)

    w_loads = []
    for i, t in enumerate(order):
        rows = pl.ds(pl.multiple_of(t * FEAT, FEAT), FEAT)
        loads = [
            pltpu.make_async_copy(wq.at[rows], w.at[rows, pl.ds(0, FEAT)], wsem.at[i, 0]),
            pltpu.make_async_copy(wk.at[rows], w.at[rows, pl.ds(FEAT, 128)], wsem.at[i, 1]),
            pltpu.make_async_copy(wv.at[rows], w.at[rows, pl.ds(FEAT + 128, 128)], wsem.at[i, 2]),
        ]
        for load in loads:
            load.start()
        w_loads.append(loads)
    load_k = pltpu.make_async_copy(ck, kvraw.at[x, 0], lsem.at[2])
    load_k.start()
    load_v = pltpu.make_async_copy(cv, kvraw.at[x, 1], lsem.at[3])
    load_v.start()
    load_tab = pltpu.make_async_copy(tab.at[ci], tabv, lsem.at[4])
    load_tab.start()
    lensb[x] = jnp.full((8, 128), lens[0], jnp.int32)
    own_h.wait()
    wide = hbuf[ti].astype(F32)
    squares = jnp.sum(wide * wide, axis=1, keepdims=True)
    ssq[ti] = jnp.broadcast_to(to_row(jnp.broadcast_to(squares, (ROWS, ROWS))), (8, 128))

    pl.semaphore_wait(barrier, len(peers))

    top_half, low_half = pl.ds(0, 64), pl.ds(64, 64)

    def h_slot(t, part):
        return hbuf.at[t, part]

    for d in range(1, 8):
        send(ssq.at[ti], ssq.at[ti], ss.at[d], sr.at[d], (ci, lax.rem(ti + d, 8)))
    send(hid.at[top_half], h_slot(ti, top_half), hs.at[0], hr.at[0], y_dev(1))
    send(hid.at[low_half], h_slot(ti, low_half), hs.at[1], hr.at[1], y_dev(3))
    send(hid, hbuf.at[ti], hs.at[4], hr.at[4], sib)
    send(hid.at[low_half], h_slot(ti, low_half), hs.at[2], hr.at[2], y_dev(1))
    send(hid.at[top_half], h_slot(ti, top_half), hs.at[3], hr.at[3], y_dev(3))
    for d in (1, 2, 3):
        send(lensb.at[x], lensb.at[x], ls.at[d], lr.at[d], x_dev(d))
    send(ck, kvraw.at[x, 0], ks.at[0], kr.at[0], x_dev(1))
    send(cv, kvraw.at[x, 1], ks.at[1], kr.at[1], x_dev(3))
    send(cv, kvraw.at[x, 1], ks.at[2], kr.at[2], x_dev(1))
    send(ck, kvraw.at[x, 0], ks.at[3], kr.at[3], x_dev(3))

    def h_wait(i, t, part=None):
        ref = hbuf.at[t] if part is None else h_slot(t, part)
        remote(ref, ref, hs.at[i], hr.at[i], sib).wait_recv()

    def h_pass(i, t, part, device):
        send(h_slot(t, part), h_slot(t, part), hs.at[i], hr.at[i], device)

    def kv_wait(i, d, which):
        ref = kvraw.at[at_x(d), which]
        remote(ref, ref, ks.at[i], kr.at[i], sib).wait_recv()

    def kv_pass(i, d, which, device):
        ref = kvraw.at[at_x(d), which]
        send(ref, ref, ks.at[i], kr.at[i], device)

    load_gain.wait()
    for d in range(1, 8):
        ref = ssq.at[lax.rem(ti + 8 - d, 8)]
        remote(ref, ref, ss.at[d], sr.at[d], sib).wait_recv()
    total = jnp.sum(ssq[...], axis=0)
    inverse = lax.rsqrt(total * (1.0 / 8192.0) + 1e-5)
    rs[...] = jnp.broadcast_to(to_column(inverse[0:1, :]), (ROWS, ROWS))

    def project(i):
        t = order[i]
        for load in w_loads[i]:
            load.wait()
        g = gbuf[pl.ds(pl.multiple_of(t * 8, 8), 8), :]
        pieces = []
        for k in range(8):
            piece = hbuf[t, :, k * 128 : (k + 1) * 128].astype(F32)
            pieces.append((piece * rs[...] * g[k : k + 1, :]).astype(BF16))
        normed = jnp.concatenate(pieces, axis=1)
        rows = pl.ds(pl.multiple_of(t * FEAT, FEAT), FEAT)
        add = jnp.dot(normed, w[rows, :], preferred_element_type=F32)
        if i == 0:
            acc[...] = add
        else:
            acc[...] += add

    project(0)
    h_wait(4, order[1])
    project(1)
    h_wait(0, at_y(3), top_half)
    h_pass(5, at_y(3), top_half, y_dev(1))
    h_wait(1, at_y(1), low_half)
    h_pass(6, at_y(1), low_half, y_dev(3))
    h_pass(7, at_y(3), top_half, sib)
    h_pass(8, at_y(1), low_half, sib)
    h_wait(2, at_y(3), low_half)
    h_pass(9, at_y(3), low_half, sib)
    project(2)
    h_wait(3, at_y(1), top_half)
    h_pass(10, at_y(1), top_half, sib)
    project(3)
    kv_wait(0, 3, 0)
    kv_pass(4, 3, 0, x_dev(1))
    kv_wait(1, 1, 1)
    kv_pass(5, 1, 1, x_dev(3))
    h_wait(7, order[4], top_half)
    h_wait(9, order[4], low_half)
    project(4)
    h_wait(8, order[5], low_half)
    h_wait(10, order[5], top_half)
    project(5)

    def prepare(position, d):
        xi = at_x(d)
        valid_len = lensb[xi][0:1, :]

        @pl.loop(0, SLOTS // 128)
        def _(step):
            part = pl.ds(pl.multiple_of(step * 128, 128), 128)
            to = pl.ds(pl.multiple_of(position * SLOTS + step * 128, 128), 128)
            row = lax.broadcasted_iota(jnp.int32, (128, 128), 0) + step * 128
            valid = row < valid_len
            first = kvraw[xi, 0, 0:16, :].astype(F32)[0:1, :]
            kp[to, :] = jnp.where(valid, kvraw[xi, 0, part, :].astype(F32), first).astype(BF16)
            vp[to, 0:128] = jnp.where(valid, kvraw[xi, 1, part, :].astype(F32), 0.0).astype(BF16)
            vp[to, 128:256] = jnp.where(valid, 1.0, 0.0).astype(BF16)

    load_k.wait()
    load_v.wait()
    prepare(0, 0)
    vp[4 * SLOTS :, 128:256] = jnp.ones((4 * ROWS, 128), BF16)

    h_wait(5, at_y(2), top_half)
    h_pass(11, at_y(2), top_half, sib)
    h_wait(6, at_y(2), low_half)
    h_pass(12, at_y(2), low_half, sib)
    project(6)
    h_wait(11, order[7], top_half)
    h_wait(12, order[7], low_half)
    load_tab.wait()
    project(7)

    def rotate(piece):
        return (piece * tabv[0] + pltpu.roll(piece, 64, 1) * tabv[1]).astype(BF16)

    own_rows = pl.ds(pl.multiple_of(4 * SLOTS + x * ROWS, ROWS), ROWS)
    kp[own_rows, :] = rotate(acc[:, FEAT : FEAT + 128])
    vp[own_rows, 0:128] = acc[:, FEAT + 128 :].astype(BF16)
    for h in range(HEADS):
        qbuf[z, h // 4, (h % 4) * 128 : (h % 4 + 1) * 128, :] = rotate(acc[:, h * 128 : (h + 1) * 128])
        if h == 3:
            for d in (1, 3, 2):
                send(qbuf.at[z, 0], qbuf.at[z, 0], qs.at[d, 0], qr.at[d, 0], z_dev(d))
            for d in (1, 3, 2):
                rows = kp.at[own_rows]
                send(rows, rows, os_.at[d, 0], or_.at[d, 0], x_dev(d))
                rows = vp.at[own_rows, pl.ds(0, 128)]
                send(rows, rows, os_.at[d, 1], or_.at[d, 1], x_dev(d))
    for d in (2, 1, 3):
        send(qbuf.at[z, 1], qbuf.at[z, 1], qs.at[d, 1], qr.at[d, 1], z_dev(d))

    def own_bias(d):
        row = lax.broadcasted_iota(jnp.int32, (ROWS, TILE), 0)
        col = lax.broadcasted_iota(jnp.int32, (ROWS, TILE), 1)
        least = 128 * (4 * (z - at_z(d)) - x)
        return jnp.where(row - col >= least, 0.0, LOW)

    def finish(state, zi, half):
        top, both = state
        denominator = both[:, 128:]
        pout[zi, half] = (both[:, :128] / denominator).astype(BF16)
        lse = top * SCALE + jnp.log(denominator)
        rows = [to_row(lse[h * 128 : (h + 1) * 128]) for h in range(4)]
        lout[zi, half] = jnp.concatenate(rows + rows, axis=0)

    def tile(q, state, i, bias=None):
        rows = slice(i * TILE, (i + 1) * TILE)
        return tile_step(q, state, kp[rows, :], vp[rows, :], bias)

    for d in (1, 2, 3):
        ref = lensb.at[at_x(4 - d)]
        remote(ref, ref, ls.at[d], lr.at[d], sib).wait_recv()
    q = qbuf[z, 0]
    state = tile(q, None, 0)
    state = tile(q, state, 1)
    kv_wait(2, 3, 1)
    prepare(1, 3)
    state = tile(q, state, 2)
    state = tile(q, state, 3)
    kv_wait(3, 1, 0)
    prepare(2, 1)
    state = tile(q, state, 4)
    state = tile(q, state, 5)
    kv_wait(4, 2, 0)
    kv_wait(5, 2, 1)
    prepare(3, 2)
    state = tile(q, state, 6)
    state = tile(q, state, 7)
    for d in (1, 2, 3):
        rows = pl.ds(pl.multiple_of(4 * SLOTS + at_x(4 - d) * ROWS, ROWS), ROWS)
        ref = kp.at[rows]
        remote(ref, ref, os_.at[d, 0], or_.at[d, 0], sib).wait_recv()
        ref = vp.at[rows, pl.ds(0, 128)]
        remote(ref, ref, os_.at[d, 1], or_.at[d, 1], sib).wait_recv()
    state = tile(q, state, 8, own_bias(0))
    finish(state, z, 0)

    def back(d, half):
        zi = at_z(d)
        return [
            remote(pout.at[zi, half], pin.at[z, half], ps.at[d, half], pr.at[d, half], z_dev(d)),
            remote(lout.at[zi, half], lin.at[z, half], es.at[d, half], er.at[d, half], z_dev(d)),
        ]

    @pl.loop(1, 8)
    def _(u):
        half = lax.div(u, 4)
        v = u + half * (7 - 2 * u)
        d = v + lax.div(v, 2) * (5 - 2 * v)
        zi = at_z(d)

        @pl.when(d != 0)
        def _():
            ref = qbuf.at[zi, half]
            remote(ref, ref, qs.at[4 - d, half], qr.at[4 - d, half], sib).wait_recv()

        q = qbuf[zi, half]
        state = None
        for i in range(8):
            state = tile(q, state, i)
        finish(tile(q, state, 8, own_bias(d)), zi, half)

        @pl.when(d != 0)
        def _():
            for copy in back(d, half):
                copy.start()

    for half in range(2):
        for d in (1, 2, 3):
            ref = pin.at[at_z(4 - d), half]
            remote(ref, ref, ps.at[d, half], pr.at[d, half], sib).wait_recv()
            ref = lin.at[at_z(4 - d), half]
            remote(ref, ref, es.at[d, half], er.at[d, half], sib).wait_recv()
        logs = [lout[z, half]] + [lin[at_z(d), half] for d in (1, 2, 3)]
        top = functools.reduce(jnp.maximum, logs)
        weights = [jnp.exp(log - top) for log in logs]
        denominator = functools.reduce(jnp.add, weights)
        weights = [weight / denominator for weight in weights]
        for h in range(4):
            rows = slice(h * 128, (h + 1) * 128)
            total = None
            for d in range(4):
                part = pout[z, half, rows, :] if d == 0 else pin[at_z(d), half, rows, :]
                term = part.astype(F32) * to_column(weights[d][h : h + 1, :])
                total = term if total is None else total + term
            head = half * 4 + h
            out[:, head * 128 : (head + 1) * 128] = total.astype(BF16)

    for copy in sends:
        copy.wait_send()
    for half in range(2):
        for d in (1, 2, 3):
            for copy in back(d, half):
                copy.wait_send()


def local(hidden, norm_gain, w_query, w_key, w_value, cache_keys, cache_values, cache_lengths):
    anywhere = pl.BlockSpec(memory_space=pl.ANY)
    tables = jnp.asarray(rotary_tables())
    dma = pltpu.SemaphoreType.DMA
    return pl.pallas_call(
        kernel,
        out_shape=jax.ShapeDtypeStruct((ROWS, FEAT), BF16),
        in_specs=[anywhere] * 7 + [pl.BlockSpec(memory_space=pltpu.SMEM), anywhere],
        out_specs=pl.BlockSpec(memory_space=pltpu.VMEM),
        scratch_shapes=[
            pltpu.VMEM((8 * FEAT, WIDTH), BF16),
            pltpu.VMEM((8, ROWS, FEAT), BF16),
            pltpu.VMEM((64, 128), F32),
            pltpu.VMEM((2, ROWS, 128), F32),
            pltpu.VMEM((8, 8, 128), F32),
            pltpu.VMEM((ROWS, ROWS), F32),
            pltpu.VMEM((ROWS, WIDTH), F32),
            pltpu.VMEM((4, 2, SLOTS, 128), BF16),
            pltpu.VMEM((4, 8, 128), jnp.int32),
            pltpu.VMEM((KEYS, 128), BF16),
            pltpu.VMEM((KEYS, 256), BF16),
            pltpu.VMEM((4, 2, HALF, 128), BF16),
            pltpu.VMEM((4, 2, HALF, 128), BF16),
            pltpu.VMEM((4, 2, HALF, 128), BF16),
            pltpu.VMEM((4, 2, 8, 128), F32),
            pltpu.VMEM((4, 2, 8, 128), F32),
            dma((8, 3)), dma((5,)),
            dma((13,)), dma((13,)),
            dma((8,)), dma((8,)),
            dma((6,)), dma((6,)),
            dma((4,)), dma((4,)),
            dma((4, 2)), dma((4, 2)),
            dma((4, 2)), dma((4, 2)),
            dma((4, 2)), dma((4, 2)),
            dma((4, 2)), dma((4, 2)),
        ],
        compiler_params=pltpu.CompilerParams(
            collective_id=0, has_side_effects=True, vmem_limit_bytes=60 * 2**20
        ),
        name="star_query",
    )(
        hidden, norm_gain.reshape(64, 128), w_query, w_key, w_value,
        cache_keys, cache_values, cache_lengths, tables,
    )


def solution(mesh):
    placed = (
        P("ctx", "tensor"),
        P(),
        P(None, "tensor"),
        P(None, "tensor"),
        P(None, "tensor"),
        P("ctx", "tensor"),
        P("ctx", "tensor"),
        P("ctx"),
    )
    return jax.shard_map(
        local, mesh=mesh, in_specs=placed, out_specs=P("ctx", "tensor"), check_vma=False
    )
```

```python
import functools

import jax
import jax.numpy as jnp
import numpy as np
from jax import lax
from jax.experimental import pallas as pl
from jax.experimental.pallas import tpu as pltpu
from jax.sharding import PartitionSpec as P

HEAD_DIM = 128
ROWS = 128
FEAT = 1024
SLOTS = 1024
HEADS = 8
HALF = 4 * ROWS
TILE = 512
KEYS = 4 * SLOTS + 4 * ROWS
WIDTH = HEADS * HEAD_DIM + 2 * HEAD_DIM
SCALE = 1.0 / HEAD_DIM**0.5
EXP2 = SCALE / float(np.log(2.0))
LOW = -1e30
MESH = pl.DeviceIdType.MESH
NT = (((1,), (1,)), ((), ()))
F32, BF16 = jnp.float32, jnp.bfloat16


def rotary_tables():
    half = HEAD_DIM // 2
    freq = 500000.0 ** (-2.0 * np.arange(half) / HEAD_DIM)
    angle = (16384 + np.arange(2048))[:, None] * freq[None, :]
    cosine, sine = np.cos(angle), np.sin(angle)
    both = np.stack(
        [np.concatenate([cosine, cosine], 1), np.concatenate([-sine, sine], 1)]
    )
    both = both.reshape(2, 16, ROWS, HEAD_DIM).transpose(1, 0, 2, 3)
    return both.astype(np.float32)


def eye():
    row = lax.broadcasted_iota(jnp.int32, (ROWS, ROWS), 0)
    col = lax.broadcasted_iota(jnp.int32, (ROWS, ROWS), 1)
    return row == col


def to_row(column):
    return jnp.sum(jnp.where(eye(), column, 0.0), axis=0, keepdims=True)


def to_column(row):
    wide = jnp.broadcast_to(row, (ROWS, ROWS))
    return jnp.sum(jnp.where(eye(), wide, 0.0), axis=1, keepdims=True)


def scores(q, keys):
    return lax.dot_general(q, keys, NT, preferred_element_type=F32)


def absorb(s, state, values, bias=None):
    if bias is not None:
        s = (s.reshape(4, ROWS, TILE) + bias[None]).reshape(HALF, TILE)
    top = jnp.max(s, axis=1, keepdims=True)
    if state is not None:
        top = jnp.maximum(state[0], top)
    p = jnp.exp2((s - top) * EXP2).astype(BF16)
    add = jnp.dot(p, values, preferred_element_type=F32)
    if state is None:
        return top, add
    return top, state[1] * jnp.exp2((state[0] - top) * EXP2) + add


def kernel(
    hid, gain, wq, wk, wv, ck, cv, lens, tab, out,
    w, hbuf, gbuf, tabv, ssq, rs, acc, kvraw, lensb, kp, vp, qbuf, pout, pin, lout, lin, mst, ost,
    wsem, lsem, hs, hr, ss, sr, ks, kr, ls, lr, os_, or_, qs, qr, ps, pr, es, er,
):
    ci, ti = lax.axis_index("ctx"), lax.axis_index("tensor")
    z, x = lax.div(ci, 4), lax.rem(ci, 4)
    y, c = lax.div(ti, 2), lax.rem(ti, 2)

    def at_y(d, other=False):
        core = 1 - c if other else c
        return 2 * lax.rem(y + d, 4) + core

    def at_x(d):
        return lax.rem(x + d, 4)

    def at_z(d):
        return lax.rem(z + d, 4)

    def x_dev(d):
        return (4 * z + at_x(d), ti)

    def z_dev(d):
        return (4 * at_z(d) + x, ti)

    def y_dev(d):
        return (ci, at_y(d))

    sib = (ci, at_y(0, True))
    sends = []

    def remote(src, dst, send_sem, recv_sem, device):
        return pltpu.make_async_remote_copy(
            src_ref=src, dst_ref=dst, send_sem=send_sem, recv_sem=recv_sem,
            device_id=device, device_id_type=MESH,
        )

    def send(*args):
        copy = remote(*args)
        copy.start()
        sends.append(copy)

    order = [at_y(0), at_y(0, True), at_y(3), at_y(1), at_y(3, True), at_y(1, True), at_y(2), at_y(2, True)]
    own_h = pltpu.make_async_copy(hid, hbuf.at[ti], lsem.at[0])
    own_h.start()
    load_gain = pltpu.make_async_copy(gain, gbuf, lsem.at[1])
    load_gain.start()

    barrier = pltpu.get_barrier_semaphore()
    peers = [(ci, lax.rem(ti + d, 8)) for d in range(1, 8)]
    peers += [x_dev(d) for d in (1, 2, 3)] + [z_dev(d) for d in (1, 2, 3)]
    for peer in peers:
        pl.semaphore_signal(barrier, inc=1, device_id=peer, device_id_type=MESH)

    w_loads = []
    for i, t in enumerate(order):
        rows = pl.ds(pl.multiple_of(t * FEAT, FEAT), FEAT)
        loads = [
            pltpu.make_async_copy(wq.at[rows], w.at[rows, pl.ds(0, FEAT)], wsem.at[i, 0]),
            pltpu.make_async_copy(wk.at[rows], w.at[rows, pl.ds(FEAT, 128)], wsem.at[i, 1]),
            pltpu.make_async_copy(wv.at[rows], w.at[rows, pl.ds(FEAT + 128, 128)], wsem.at[i, 2]),
        ]
        for load in loads:
            load.start()
        w_loads.append(loads)
    load_k = pltpu.make_async_copy(ck, kvraw.at[x, 0], lsem.at[2])
    load_k.start()
    load_v = pltpu.make_async_copy(cv, kvraw.at[x, 1], lsem.at[3])
    load_v.start()
    load_tab = pltpu.make_async_copy(tab.at[ci], tabv, lsem.at[4])
    load_tab.start()
    lensb[x] = jnp.full((8, 128), lens[0], jnp.int32)
    own_h.wait()
    wide = hbuf[ti].astype(F32)
    squares = jnp.sum(wide * wide, axis=1, keepdims=True)
    ssq[ti] = jnp.broadcast_to(to_row(jnp.broadcast_to(squares, (ROWS, ROWS))), (8, 128))

    pl.semaphore_wait(barrier, len(peers))

    def h_ref(t, first, count):
        return hbuf.at[t, :, pl.ds(256 * first, 256 * count)]

    def h_send(i, t, first, count, device):
        send(h_ref(t, first, count), h_ref(t, first, count), hs.at[i], hr.at[i], device)

    def h_wait(i, t, first, count):
        ref = h_ref(t, first, count)
        remote(ref, ref, hs.at[i], hr.at[i], sib).wait_recv()

    for d in range(1, 8):
        send(ssq.at[ti], ssq.at[ti], ss.at[d], sr.at[d], (ci, lax.rem(ti + d, 8)))
    for k in range(4):
        h_send(k, ti, k, 1, y_dev(1))
        h_send(4 + k, ti, (k + 2) % 4, 1, y_dev(3))
        if k == 0:
            h_send(12, ti, 0, 4, sib)
    for d in (1, 2, 3):
        send(lensb.at[x], lensb.at[x], ls.at[d], lr.at[d], x_dev(d))
    send(ck, kvraw.at[x, 0], ks.at[0], kr.at[0], x_dev(1))
    send(cv, kvraw.at[x, 1], ks.at[1], kr.at[1], x_dev(3))
    send(cv, kvraw.at[x, 1], ks.at[2], kr.at[2], x_dev(1))
    send(ck, kvraw.at[x, 0], ks.at[3], kr.at[3], x_dev(3))

    def kv_wait(i, d, which):
        ref = kvraw.at[at_x(d), which]
        remote(ref, ref, ks.at[i], kr.at[i], sib).wait_recv()

    def kv_pass(i, d, which, device):
        ref = kvraw.at[at_x(d), which]
        send(ref, ref, ks.at[i], kr.at[i], device)

    load_gain.wait()
    for d in range(1, 8):
        ref = ssq.at[lax.rem(ti + 8 - d, 8)]
        remote(ref, ref, ss.at[d], sr.at[d], sib).wait_recv()
    total = jnp.sum(ssq[...], axis=0)
    inverse = lax.rsqrt(total * (1.0 / 8192.0) + 1e-5)
    rs[...] = jnp.broadcast_to(to_column(inverse[0:1, :]), (ROWS, ROWS))

    def prepare(position, d):
        xi = at_x(d)
        valid_len = lensb[xi][0:1, :]

        @pl.loop(0, SLOTS // 128)
        def _(step):
            part = pl.ds(pl.multiple_of(step * 128, 128), 128)
            to = pl.ds(pl.multiple_of(position * SLOTS + step * 128, 128), 128)
            row = lax.broadcasted_iota(jnp.int32, (128, 128), 0) + step * 128
            valid = row < valid_len
            first = kvraw[xi, 0, 0:16, :].astype(F32)[0:1, :]
            kp[to, :] = jnp.where(valid, kvraw[xi, 0, part, :].astype(F32), first).astype(BF16)
            vp[to, 0:128] = jnp.where(valid, kvraw[xi, 1, part, :].astype(F32), 0.0).astype(BF16)
            vp[to, 128:256] = jnp.where(valid, 1.0, 0.0).astype(BF16)

    def project(i, first=0, count=4):
        t = order[i]
        g = gbuf[pl.ds(pl.multiple_of(t * 8, 8), 8), :]
        pieces = []
        for k in range(2 * first, 2 * (first + count)):
            piece = hbuf[t, :, k * 128 : (k + 1) * 128].astype(F32)
            pieces.append((piece * rs[...] * g[k : k + 1, :]).astype(BF16))
        normed = jnp.concatenate(pieces, axis=1)
        rows = pl.ds(pl.multiple_of(t * FEAT + first * 256, 256), count * 256)
        return jnp.dot(normed, w[rows, :], preferred_element_type=F32)

    def loaded(*chunks):
        for i in chunks:
            for load in w_loads[i]:
                load.wait()

    left, right, far = at_y(3), at_y(1), at_y(2)
    loaded(0, 1)
    acc[...] = project(0)
    h_wait(12, order[1], 0, 4)
    acc[...] += project(1)
    for k in (0, 1):
        h_wait(k, left, k, 1)
        h_send(8 + k, left, k, 1, y_dev(1))
        h_wait(4 + k, right, 2 + k, 1)
        h_send(10 + k, right, 2 + k, 1, y_dev(3))
    h_send(13, left, 0, 2, sib)
    h_send(14, right, 2, 2, sib)
    loaded(2, 3)
    acc[...] += project(2, 0, 2) + project(3, 2, 2)
    h_wait(13, order[4], 0, 2)
    h_wait(14, order[5], 2, 2)
    loaded(4, 5)
    acc[...] += project(4, 0, 2) + project(5, 2, 2)
    for k in (2, 3):
        h_wait(k, left, k, 1)
        h_wait(4 + k, right, k - 2, 1)
    h_send(15, left, 2, 2, sib)
    h_send(16, right, 0, 2, sib)
    acc[...] += project(2, 2, 2) + project(3, 0, 2)
    kv_wait(0, 3, 0)
    kv_pass(4, 3, 0, x_dev(1))
    kv_wait(1, 1, 1)
    kv_pass(5, 1, 1, x_dev(3))
    h_wait(15, order[4], 2, 2)
    h_wait(16, order[5], 0, 2)
    acc[...] += project(4, 2, 2) + project(5, 0, 2)
    h_wait(8, far, 0, 1)
    h_send(17, far, 0, 1, sib)
    h_wait(10, far, 2, 1)
    h_send(18, far, 2, 1, sib)
    loaded(6, 7)
    acc[...] += project(6, 0, 1) + project(6, 2, 1)
    load_k.wait()
    load_v.wait()
    prepare(0, 0)
    vp[4 * SLOTS :, 128:256] = jnp.ones((4 * ROWS, 128), BF16)
    load_tab.wait()
    h_wait(9, far, 1, 1)
    h_send(19, far, 1, 1, sib)
    h_wait(11, far, 3, 1)
    h_send(20, far, 3, 1, sib)
    h_wait(17, order[7], 0, 1)
    h_wait(18, order[7], 2, 1)
    acc[...] += project(6, 1, 1) + project(6, 3, 1) + project(7, 0, 1) + project(7, 2, 1)
    h_wait(19, order[7], 1, 1)
    h_wait(20, order[7], 3, 1)
    acc[...] += project(7, 1, 1) + project(7, 3, 1)

    def rotate(piece):
        return (piece * tabv[0] + pltpu.roll(piece, 64, 1) * tabv[1]).astype(BF16)

    own_rows = pl.ds(pl.multiple_of(4 * SLOTS + x * ROWS, ROWS), ROWS)
    kp[own_rows, :] = rotate(acc[:, FEAT : FEAT + 128])
    vp[own_rows, 0:128] = acc[:, FEAT + 128 :].astype(BF16)
    for d in (1, 3, 2):
        rows = kp.at[own_rows]
        send(rows, rows, os_.at[d, 0], or_.at[d, 0], x_dev(d))
        rows = vp.at[own_rows, pl.ds(0, 128)]
        send(rows, rows, os_.at[d, 1], or_.at[d, 1], x_dev(d))

    def q_send(d, half):
        send(qbuf.at[z, half], qbuf.at[z, half], qs.at[d, half], qr.at[d, half], z_dev(d))

    for h in range(HEADS):
        qbuf[z, h // 4, (h % 4) * 128 : (h % 4 + 1) * 128, :] = rotate(acc[:, h * 128 : (h + 1) * 128])
        if h == 3:
            q_send(1, 0)
            q_send(3, 0)

    def own_bias(d):
        row = lax.broadcasted_iota(jnp.int32, (ROWS, TILE), 0)
        col = lax.broadcasted_iota(jnp.int32, (ROWS, TILE), 1)
        least = 128 * (4 * (z - at_z(d)) - x)
        return jnp.where(row - col >= least, 0.0, LOW)

    def finish(state, zi, half):
        top, both = state
        denominator = both[:, 128:]
        pout[zi, half] = (both[:, :128] / denominator).astype(BF16)
        lse = top * SCALE + jnp.log(denominator)
        rows = [to_row(lse[h * 128 : (h + 1) * 128]) for h in range(4)]
        lout[zi, half] = jnp.concatenate(rows + rows, axis=0)

    def run(q, state, tiles, bias=None):
        def rows(i):
            return slice(i * TILE, (i + 1) * TILE)

        s = scores(q, kp[rows(tiles[0]), :])
        for n, i in enumerate(tiles):
            later = scores(q, kp[rows(tiles[n + 1]), :]) if n + 1 < len(tiles) else None
            state = absorb(s, state, vp[rows(i), :], bias if i == 8 else None)
            s = later
        return state

    def keep(half, state):
        mst[half] = jnp.broadcast_to(state[0], (HALF, 128))
        ost[half] = state[1]

    def kept(half):
        return mst[half][:, 0:1], ost[half]

    for d in (1, 2, 3):
        ref = lensb.at[at_x(4 - d)]
        remote(ref, ref, ls.at[d], lr.at[d], sib).wait_recv()
    kv_wait(2, 3, 1)
    prepare(1, 3)
    kv_wait(3, 1, 0)
    prepare(2, 1)
    keep(0, run(qbuf[z, 0], None, range(6)))
    q_send(2, 0)
    q_send(2, 1)
    keep(1, run(qbuf[z, 1], None, range(6)))
    q_send(1, 1)
    q_send(3, 1)
    kv_wait(4, 2, 0)
    kv_wait(5, 2, 1)
    prepare(3, 2)
    keep(0, run(qbuf[z, 0], kept(0), (6, 7)))
    for d in (1, 2, 3):
        rows = pl.ds(pl.multiple_of(4 * SLOTS + at_x(4 - d) * ROWS, ROWS), ROWS)
        ref = kp.at[rows]
        remote(ref, ref, os_.at[d, 0], or_.at[d, 0], sib).wait_recv()
        ref = vp.at[rows, pl.ds(0, 128)]
        remote(ref, ref, os_.at[d, 1], or_.at[d, 1], sib).wait_recv()

    def back(d, half):
        zi = at_z(d)
        return [
            remote(pout.at[zi, half], pin.at[z, half], ps.at[d, half], pr.at[d, half], z_dev(d)),
            remote(lout.at[zi, half], lin.at[z, half], es.at[d, half], er.at[d, half], z_dev(d)),
        ]

    @pl.loop(0, 6)
    def _(u):
        half = lax.div(u, 3)
        v = 1 + u + half * (5 - 2 * u)
        d = v + lax.div(v, 2) * (5 - 2 * v)
        zi = at_z(d)
        ref = qbuf.at[zi, half]
        remote(ref, ref, qs.at[4 - d, half], qr.at[4 - d, half], sib).wait_recv()
        finish(run(qbuf[zi, half], None, range(9), own_bias(d)), zi, half)
        for copy in back(d, half):
            copy.start()

    finish(run(qbuf[z, 0], kept(0), (8,), own_bias(0)), z, 0)
    finish(run(qbuf[z, 1], kept(1), (6, 7, 8), own_bias(0)), z, 1)

    for half in range(2):
        for d in (1, 2, 3):
            ref = pin.at[at_z(4 - d), half]
            remote(ref, ref, ps.at[d, half], pr.at[d, half], sib).wait_recv()
            ref = lin.at[at_z(4 - d), half]
            remote(ref, ref, es.at[d, half], er.at[d, half], sib).wait_recv()
        logs = [lout[z, half]] + [lin[at_z(d), half] for d in (1, 2, 3)]
        top = functools.reduce(jnp.maximum, logs)
        weights = [jnp.exp(log - top) for log in logs]
        denominator = functools.reduce(jnp.add, weights)
        weights = [weight / denominator for weight in weights]
        for h in range(4):
            rows = slice(h * 128, (h + 1) * 128)
            total = None
            for d in range(4):
                part = pout[z, half, rows, :] if d == 0 else pin[at_z(d), half, rows, :]
                term = part.astype(F32) * to_column(weights[d][h : h + 1, :])
                total = term if total is None else total + term
            head = half * 4 + h
            out[:, head * 128 : (head + 1) * 128] = total.astype(BF16)

    for copy in sends:
        copy.wait_send()
    for half in range(2):
        for d in (1, 2, 3):
            for copy in back(d, half):
                copy.wait_send()


def local(hidden, norm_gain, w_query, w_key, w_value, cache_keys, cache_values, cache_lengths):
    anywhere = pl.BlockSpec(memory_space=pl.ANY)
    tables = jnp.asarray(rotary_tables())
    dma = pltpu.SemaphoreType.DMA
    return pl.pallas_call(
        kernel,
        out_shape=jax.ShapeDtypeStruct((ROWS, FEAT), BF16),
        in_specs=[anywhere] * 7 + [pl.BlockSpec(memory_space=pltpu.SMEM), anywhere],
        out_specs=pl.BlockSpec(memory_space=pltpu.VMEM),
        scratch_shapes=[
            pltpu.VMEM((8 * FEAT, WIDTH), BF16),
            pltpu.VMEM((8, ROWS, FEAT), BF16),
            pltpu.VMEM((64, 128), F32),
            pltpu.VMEM((2, ROWS, 128), F32),
            pltpu.VMEM((8, 8, 128), F32),
            pltpu.VMEM((ROWS, ROWS), F32),
            pltpu.VMEM((ROWS, WIDTH), F32),
            pltpu.VMEM((4, 2, SLOTS, 128), BF16),
            pltpu.VMEM((4, 8, 128), jnp.int32),
            pltpu.VMEM((KEYS, 128), BF16),
            pltpu.VMEM((KEYS, 256), BF16),
            pltpu.VMEM((4, 2, HALF, 128), BF16),
            pltpu.VMEM((4, 2, HALF, 128), BF16),
            pltpu.VMEM((4, 2, HALF, 128), BF16),
            pltpu.VMEM((4, 2, 8, 128), F32),
            pltpu.VMEM((4, 2, 8, 128), F32),
            pltpu.VMEM((2, HALF, 128), F32),
            pltpu.VMEM((2, HALF, 256), F32),
            dma((8, 3)), dma((5,)),
            dma((21,)), dma((21,)),
            dma((8,)), dma((8,)),
            dma((6,)), dma((6,)),
            dma((4,)), dma((4,)),
            dma((4, 2)), dma((4, 2)),
            dma((4, 2)), dma((4, 2)),
            dma((4, 2)), dma((4, 2)),
            dma((4, 2)), dma((4, 2)),
        ],
        compiler_params=pltpu.CompilerParams(
            collective_id=0, has_side_effects=True, vmem_limit_bytes=60 * 2**20
        ),
        name="star_query",
    )(
        hidden, norm_gain.reshape(64, 128), w_query, w_key, w_value,
        cache_keys, cache_values, cache_lengths, tables,
    )


def solution(mesh):
    placed = (
        P("ctx", "tensor"),
        P(),
        P(None, "tensor"),
        P(None, "tensor"),
        P(None, "tensor"),
        P("ctx", "tensor"),
        P("ctx", "tensor"),
        P("ctx"),
    )
    return jax.shard_map(
        local, mesh=mesh, in_specs=placed, out_specs=P("ctx", "tensor"), check_vma=False
    )
```

```python
import functools

import jax
import jax.numpy as jnp
import numpy as np
from jax import lax
from jax.experimental import pallas as pl
from jax.experimental.pallas import tpu as pltpu
from jax.sharding import PartitionSpec as P

HEAD_DIM = 128
ROWS = 128
FEAT = 1024
SLOTS = 1024
HEADS = 8
HALF = 4 * ROWS
TILE = 512
KEYS = 4 * SLOTS + 2 * TILE
WIDTH = HEADS * HEAD_DIM + 2 * HEAD_DIM
SCALE = 1.0 / HEAD_DIM**0.5
EXP2 = SCALE / float(np.log(2.0))
LOW = -1e30
MESH = pl.DeviceIdType.MESH
NT = (((1,), (1,)), ((), ()))
F32, BF16 = jnp.float32, jnp.bfloat16


def rotary_tables():
    half = HEAD_DIM // 2
    freq = 500000.0 ** (-2.0 * np.arange(half) / HEAD_DIM)
    angle = (16384 + np.arange(2048))[:, None] * freq[None, :]
    cosine, sine = np.cos(angle), np.sin(angle)
    both = np.stack(
        [np.concatenate([cosine, cosine], 1), np.concatenate([-sine, sine], 1)]
    )
    both = both.reshape(2, 16, ROWS, HEAD_DIM).transpose(1, 0, 2, 3)
    return both.astype(np.float32)


def eye():
    row = lax.broadcasted_iota(jnp.int32, (ROWS, ROWS), 0)
    col = lax.broadcasted_iota(jnp.int32, (ROWS, ROWS), 1)
    return row == col


def to_row(column):
    return jnp.sum(jnp.where(eye(), column, 0.0), axis=0, keepdims=True)


def to_column(row):
    wide = jnp.broadcast_to(row, (ROWS, ROWS))
    return jnp.sum(jnp.where(eye(), wide, 0.0), axis=1, keepdims=True)


def scores(q, keys):
    return lax.dot_general(q, keys, NT, preferred_element_type=F32)


def absorb(s, state, values, bias=None):
    if bias is not None:
        s = (s.reshape(4, ROWS, TILE) + bias[None]).reshape(HALF, TILE)
    top = jnp.max(s, axis=1, keepdims=True)
    if state is not None:
        top = jnp.maximum(state[0], top)
    p = jnp.exp2((s - top) * EXP2).astype(BF16)
    add = jnp.dot(p, values, preferred_element_type=F32)
    if state is None:
        return top, add
    return top, state[1] * jnp.exp2((state[0] - top) * EXP2) + add


def kernel(
    hid, gain, wq, wk, wv, ck, cv, lens, tab, out,
    w, hbuf, gbuf, tabv, ssq, rs, acc, kvraw, lensb, kp, vp, qbuf, pout, pin, lout, lin, mst, ost,
    wsem, lsem, hs, hr, ss, sr, ks, kr, ls, lr, os_, or_, qs, qr, ps, pr, es, er,
):
    ci, ti = lax.axis_index("ctx"), lax.axis_index("tensor")
    z, x = lax.div(ci, 4), lax.rem(ci, 4)
    y, c = lax.div(ti, 2), lax.rem(ti, 2)

    def at_y(d, other=False):
        core = 1 - c if other else c
        return 2 * lax.rem(y + d, 4) + core

    def at_x(d):
        return lax.rem(x + d, 4)

    def at_z(d):
        return lax.rem(z + d, 4)

    def x_dev(d):
        return (4 * z + at_x(d), ti)

    def z_dev(d):
        return (4 * at_z(d) + x, ti)

    def y_dev(d):
        return (ci, at_y(d))

    sib = (ci, at_y(0, True))
    sends = []

    def remote(src, dst, send_sem, recv_sem, device):
        return pltpu.make_async_remote_copy(
            src_ref=src, dst_ref=dst, send_sem=send_sem, recv_sem=recv_sem,
            device_id=device, device_id_type=MESH,
        )

    def send(*args):
        copy = remote(*args)
        copy.start()
        sends.append(copy)

    order = [at_y(0), at_y(0, True), at_y(3), at_y(1), at_y(3, True), at_y(1, True), at_y(2), at_y(2, True)]
    own_h = pltpu.make_async_copy(hid, hbuf.at[ti], lsem.at[0])
    own_h.start()
    load_gain = pltpu.make_async_copy(gain, gbuf, lsem.at[1])
    load_gain.start()

    barrier = pltpu.get_barrier_semaphore()
    peers = [(ci, lax.rem(ti + d, 8)) for d in range(1, 8)]
    peers += [x_dev(d) for d in (1, 2, 3)] + [z_dev(d) for d in (1, 2, 3)]
    for peer in peers:
        pl.semaphore_signal(barrier, inc=1, device_id=peer, device_id_type=MESH)

    w_loads = []
    for i, t in enumerate(order):
        rows = pl.ds(pl.multiple_of(t * FEAT, FEAT), FEAT)
        loads = [
            pltpu.make_async_copy(wq.at[rows], w.at[rows, pl.ds(0, FEAT)], wsem.at[i, 0]),
            pltpu.make_async_copy(wk.at[rows], w.at[rows, pl.ds(FEAT, 128)], wsem.at[i, 1]),
            pltpu.make_async_copy(wv.at[rows], w.at[rows, pl.ds(FEAT + 128, 128)], wsem.at[i, 2]),
        ]
        for load in loads:
            load.start()
        w_loads.append(loads)
    load_k = pltpu.make_async_copy(ck, kvraw.at[x, 0], lsem.at[2])
    load_k.start()
    load_v = pltpu.make_async_copy(cv, kvraw.at[x, 1], lsem.at[3])
    load_v.start()
    load_tab = pltpu.make_async_copy(tab.at[ci], tabv, lsem.at[4])
    load_tab.start()
    lensb[x] = jnp.full((8, 128), lens[0], jnp.int32)
    own_h.wait()
    wide = hbuf[ti].astype(F32)
    squares = jnp.sum(wide * wide, axis=1, keepdims=True)
    ssq[ti] = jnp.broadcast_to(to_row(jnp.broadcast_to(squares, (ROWS, ROWS))), (8, 128))

    pl.semaphore_wait(barrier, len(peers))

    def h_ref(t, first, count):
        return hbuf.at[t, :, pl.ds(256 * first, 256 * count)]

    def h_send(i, t, first, count, device):
        send(h_ref(t, first, count), h_ref(t, first, count), hs.at[i], hr.at[i], device)

    def h_wait(i, t, first, count):
        ref = h_ref(t, first, count)
        remote(ref, ref, hs.at[i], hr.at[i], sib).wait_recv()

    for d in range(1, 8):
        send(ssq.at[ti], ssq.at[ti], ss.at[d], sr.at[d], (ci, lax.rem(ti + d, 8)))
    for k in range(4):
        h_send(k, ti, k, 1, y_dev(1))
        h_send(4 + k, ti, (k + 2) % 4, 1, y_dev(3))
        if k == 0:
            h_send(12, ti, 0, 4, sib)
    for d in (1, 2, 3):
        send(lensb.at[x], lensb.at[x], ls.at[d], lr.at[d], x_dev(d))
    send(ck, kvraw.at[x, 0], ks.at[0], kr.at[0], x_dev(1))
    send(cv, kvraw.at[x, 1], ks.at[1], kr.at[1], x_dev(3))
    send(cv, kvraw.at[x, 1], ks.at[2], kr.at[2], x_dev(1))
    send(ck, kvraw.at[x, 0], ks.at[3], kr.at[3], x_dev(3))

    def kv_wait(i, d, which):
        ref = kvraw.at[at_x(d), which]
        remote(ref, ref, ks.at[i], kr.at[i], sib).wait_recv()

    def kv_pass(i, d, which, device):
        ref = kvraw.at[at_x(d), which]
        send(ref, ref, ks.at[i], kr.at[i], device)

    load_gain.wait()
    for d in range(1, 8):
        ref = ssq.at[lax.rem(ti + 8 - d, 8)]
        remote(ref, ref, ss.at[d], sr.at[d], sib).wait_recv()
    total = jnp.sum(ssq[...], axis=0)
    inverse = lax.rsqrt(total * (1.0 / 8192.0) + 1e-5)
    rs[...] = jnp.broadcast_to(to_column(inverse[0:1, :]), (ROWS, ROWS))

    def prepare(position, d):
        xi = at_x(d)
        valid_len = lensb[xi][0:1, :]

        @pl.loop(0, SLOTS // 128)
        def _(step):
            part = pl.ds(pl.multiple_of(step * 128, 128), 128)
            to = pl.ds(pl.multiple_of(position * SLOTS + step * 128, 128), 128)
            row = lax.broadcasted_iota(jnp.int32, (128, 128), 0) + step * 128
            valid = row < valid_len
            first = kvraw[xi, 0, 0:16, :].astype(F32)[0:1, :]
            kp[to, :] = jnp.where(valid, kvraw[xi, 0, part, :].astype(F32), first).astype(BF16)
            vp[to, 0:128] = jnp.where(valid, kvraw[xi, 1, part, :].astype(F32), 0.0).astype(BF16)
            vp[to, 128:256] = jnp.where(valid, 1.0, 0.0).astype(BF16)

    def project(i, first=0, count=4):
        t = order[i]
        g = gbuf[pl.ds(pl.multiple_of(t * 8, 8), 8), :]
        pieces = []
        for k in range(2 * first, 2 * (first + count)):
            piece = hbuf[t, :, k * 128 : (k + 1) * 128].astype(F32)
            pieces.append((piece * rs[...] * g[k : k + 1, :]).astype(BF16))
        normed = jnp.concatenate(pieces, axis=1)
        rows = pl.ds(pl.multiple_of(t * FEAT + first * 256, 256), count * 256)
        return jnp.dot(normed, w[rows, :], preferred_element_type=F32)

    def loaded(*chunks):
        for i in chunks:
            for load in w_loads[i]:
                load.wait()

    left, right, far = at_y(3), at_y(1), at_y(2)
    loaded(0, 1)
    acc[...] = project(0)
    h_wait(12, order[1], 0, 4)
    acc[...] += project(1)
    for k in (0, 1):
        h_wait(k, left, k, 1)
        h_send(8 + k, left, k, 1, y_dev(1))
        h_wait(4 + k, right, 2 + k, 1)
        h_send(10 + k, right, 2 + k, 1, y_dev(3))
    h_send(13, left, 0, 2, sib)
    h_send(14, right, 2, 2, sib)
    loaded(2, 3)
    acc[...] += project(2, 0, 2) + project(3, 2, 2)
    h_wait(13, order[4], 0, 2)
    h_wait(14, order[5], 2, 2)
    loaded(4, 5)
    acc[...] += project(4, 0, 2) + project(5, 2, 2)
    for k in (2, 3):
        h_wait(k, left, k, 1)
        h_wait(4 + k, right, k - 2, 1)
    h_send(15, left, 2, 2, sib)
    h_send(16, right, 0, 2, sib)
    acc[...] += project(2, 2, 2) + project(3, 0, 2)
    h_wait(15, order[4], 2, 2)
    h_wait(16, order[5], 0, 2)
    acc[...] += project(4, 2, 2) + project(5, 0, 2)
    h_wait(8, far, 0, 1)
    h_send(17, far, 0, 1, sib)
    h_wait(10, far, 2, 1)
    h_send(18, far, 2, 1, sib)
    loaded(6, 7)
    acc[...] += project(6, 0, 1) + project(6, 2, 1)
    load_k.wait()
    load_v.wait()
    prepare(0, 0)
    vp[4 * SLOTS : 4 * SLOTS + TILE, 128:256] = jnp.ones((TILE, 128), BF16)
    vp[4 * SLOTS + TILE :, :] = jnp.zeros((TILE, 256), BF16)
    kp[4 * SLOTS + TILE :, :] = jnp.broadcast_to(kvraw[x, 0, 0:16, :].astype(F32)[0:1, :], (TILE, 128)).astype(BF16)
    load_tab.wait()
    h_wait(9, far, 1, 1)
    h_send(19, far, 1, 1, sib)
    h_wait(11, far, 3, 1)
    h_send(20, far, 3, 1, sib)
    h_wait(17, order[7], 0, 1)
    h_wait(18, order[7], 2, 1)
    acc[...] += project(6, 1, 1) + project(6, 3, 1) + project(7, 0, 1) + project(7, 2, 1)
    h_wait(19, order[7], 1, 1)
    h_wait(20, order[7], 3, 1)
    acc[...] += project(7, 1, 1) + project(7, 3, 1)

    def rotate(piece):
        return (piece * tabv[0] + pltpu.roll(piece, 64, 1) * tabv[1]).astype(BF16)

    own_rows = pl.ds(pl.multiple_of(4 * SLOTS + x * ROWS, ROWS), ROWS)
    kp[own_rows, :] = rotate(acc[:, FEAT : FEAT + 128])
    vp[own_rows, 0:128] = acc[:, FEAT + 128 :].astype(BF16)
    for d in (1, 3, 2):
        rows = kp.at[own_rows]
        send(rows, rows, os_.at[d, 0], or_.at[d, 0], x_dev(d))
        rows = vp.at[own_rows, pl.ds(0, 128)]
        send(rows, rows, os_.at[d, 1], or_.at[d, 1], x_dev(d))

    def q_send(d, half):
        send(qbuf.at[z, half], qbuf.at[z, half], qs.at[d, half], qr.at[d, half], z_dev(d))

    for h in range(HEADS):
        qbuf[z, h // 4, (h % 4) * 128 : (h % 4 + 1) * 128, :] = rotate(acc[:, h * 128 : (h + 1) * 128])
        if h == 3:
            q_send(1, 0)
            q_send(3, 0)

    def own_bias():
        row = lax.broadcasted_iota(jnp.int32, (ROWS, TILE), 0)
        col = lax.broadcasted_iota(jnp.int32, (ROWS, TILE), 1)
        return jnp.where(row - col >= -128 * x, 0.0, LOW)

    def finish(state, zi, half):
        top, both = state
        denominator = both[:, 128:]
        pout[zi, half] = (both[:, :128] / denominator).astype(BF16)
        tops = jnp.broadcast_to(top, (HALF, 128))
        parts = [slice(h * 128, (h + 1) * 128) for h in range(4)]
        top_rows = jnp.concatenate([to_row(tops[part]) for part in parts] * 2, axis=0)
        sum_rows = jnp.concatenate([to_row(denominator[part]) for part in parts] * 2, axis=0)
        lout[zi, half] = top_rows * SCALE + jnp.log(sum_rows)

    def run(*units):
        steps = [(unit, tile) for unit in units for tile in unit[2]]

        def rows(tile):
            return slice(tile * TILE, (tile + 1) * TILE) if isinstance(tile, int) else tile

        def ahead(step):
            unit, tile = step
            return scores(unit[0], kp[rows(tile), :])

        s = ahead(steps[0])
        state = None
        for n, (unit, tile) in enumerate(steps):
            later = ahead(steps[n + 1]) if n + 1 < len(steps) else None
            if n == 0 or steps[n - 1][0] is not unit:
                state = unit[1]
            state = absorb(s, state, vp[rows(tile), :], own_bias() if tile == 8 else None)
            s = later
            if n + 1 == len(steps) or steps[n + 1][0] is not unit:
                unit[3](state)

    def keep(half, state):
        mst[half] = jnp.broadcast_to(state[0], (HALF, 128))
        ost[half] = state[1]

    def kept(half):
        return mst[half][:, 0:1], ost[half]

    for d in (1, 2, 3):
        ref = lensb.at[at_x(4 - d)]
        remote(ref, ref, ls.at[d], lr.at[d], sib).wait_recv()
    kv_wait(0, 3, 0)
    kv_pass(4, 3, 0, x_dev(1))
    kv_wait(1, 1, 1)
    kv_pass(5, 1, 1, x_dev(3))
    kv_wait(2, 3, 1)
    prepare(1, 3)
    kv_wait(3, 1, 0)
    prepare(2, 1)
    run((qbuf[z, 0], None, range(6), functools.partial(keep, 0)))
    q_send(2, 0)
    q_send(2, 1)
    run((qbuf[z, 1], None, range(6), functools.partial(keep, 1)))
    q_send(1, 1)
    q_send(3, 1)

    def back(d, half):
        zi = at_z(d)
        return [
            remote(pout.at[zi, half], pin.at[z, half], ps.at[d, half], pr.at[d, half], z_dev(d)),
            remote(lout.at[zi, half], lin.at[z, half], es.at[d, half], er.at[d, half], z_dev(d)),
        ]

    def end(d, half):
        def call(state):
            finish(state, at_z(d), half)
            for copy in back(d, half):
                copy.start()

        return call

    def q_wait(d, half):
        ref = qbuf.at[at_z(d), half]
        remote(ref, ref, qs.at[4 - d, half], qr.at[4 - d, half], sib).wait_recv()

    def last(d):
        return pl.ds(pl.multiple_of(4 * SLOTS + TILE * lax.div(z + d, 4), TILE), TILE)

    def unit(d, half):
        return (qbuf[at_z(d), half], None, [*range(8), last(d)], end(d, half))

    q_wait(1, 0)
    q_wait(3, 0)
    run(
        (qbuf[at_z(1), 0], None, range(6), functools.partial(keep, 2)),
        (qbuf[at_z(3), 0], None, range(6), functools.partial(keep, 3)),
    )
    kv_wait(4, 2, 0)
    kv_wait(5, 2, 1)
    prepare(3, 2)
    for d in (1, 2, 3):
        rows = pl.ds(pl.multiple_of(4 * SLOTS + at_x(4 - d) * ROWS, ROWS), ROWS)
        ref = kp.at[rows]
        remote(ref, ref, os_.at[d, 0], or_.at[d, 0], sib).wait_recv()
        ref = vp.at[rows, pl.ds(0, 128)]
        remote(ref, ref, os_.at[d, 1], or_.at[d, 1], sib).wait_recv()
    run(
        (qbuf[at_z(1), 0], kept(2), [6, 7, last(1)], end(1, 0)),
        (qbuf[at_z(3), 0], kept(3), [6, 7, last(3)], end(3, 0)),
    )
    q_wait(2, 0)
    q_wait(2, 1)
    run(unit(2, 0), unit(2, 1))
    q_wait(1, 1)
    q_wait(3, 1)
    run(unit(1, 1), unit(3, 1))

    run(
        (qbuf[z, 0], kept(0), [6, 7, 8], lambda state: finish(state, z, 0)),
        (qbuf[z, 1], kept(1), [6, 7, 8], lambda state: finish(state, z, 1)),
    )

    for half in range(2):
        for d in (1, 2, 3):
            ref = pin.at[at_z(4 - d), half]
            remote(ref, ref, ps.at[d, half], pr.at[d, half], sib).wait_recv()
            ref = lin.at[at_z(4 - d), half]
            remote(ref, ref, es.at[d, half], er.at[d, half], sib).wait_recv()
        logs = [lout[z, half]] + [lin[at_z(d), half] for d in (1, 2, 3)]
        top = functools.reduce(jnp.maximum, logs)
        weights = [jnp.exp(log - top) for log in logs]
        denominator = functools.reduce(jnp.add, weights)
        weights = [weight / denominator for weight in weights]
        for h in range(4):
            rows = slice(h * 128, (h + 1) * 128)
            total = None
            for d in range(4):
                part = pout[z, half, rows, :] if d == 0 else pin[at_z(d), half, rows, :]
                term = part.astype(F32) * to_column(weights[d][h : h + 1, :])
                total = term if total is None else total + term
            head = half * 4 + h
            out[:, head * 128 : (head + 1) * 128] = total.astype(BF16)

    for copy in sends:
        copy.wait_send()
    for half in range(2):
        for d in (1, 2, 3):
            for copy in back(d, half):
                copy.wait_send()


def local(hidden, norm_gain, w_query, w_key, w_value, cache_keys, cache_values, cache_lengths):
    anywhere = pl.BlockSpec(memory_space=pl.ANY)
    tables = jnp.asarray(rotary_tables())
    dma = pltpu.SemaphoreType.DMA
    return pl.pallas_call(
        kernel,
        out_shape=jax.ShapeDtypeStruct((ROWS, FEAT), BF16),
        in_specs=[anywhere] * 7 + [pl.BlockSpec(memory_space=pltpu.SMEM), anywhere],
        out_specs=pl.BlockSpec(memory_space=pltpu.VMEM),
        scratch_shapes=[
            pltpu.VMEM((8 * FEAT, WIDTH), BF16),
            pltpu.VMEM((8, ROWS, FEAT), BF16),
            pltpu.VMEM((64, 128), F32),
            pltpu.VMEM((2, ROWS, 128), F32),
            pltpu.VMEM((8, 8, 128), F32),
            pltpu.VMEM((ROWS, ROWS), F32),
            pltpu.VMEM((ROWS, WIDTH), F32),
            pltpu.VMEM((4, 2, SLOTS, 128), BF16),
            pltpu.VMEM((4, 8, 128), jnp.int32),
            pltpu.VMEM((KEYS, 128), BF16),
            pltpu.VMEM((KEYS, 256), BF16),
            pltpu.VMEM((4, 2, HALF, 128), BF16),
            pltpu.VMEM((4, 2, HALF, 128), BF16),
            pltpu.VMEM((4, 2, HALF, 128), BF16),
            pltpu.VMEM((4, 2, 8, 128), F32),
            pltpu.VMEM((4, 2, 8, 128), F32),
            pltpu.VMEM((4, HALF, 128), F32),
            pltpu.VMEM((4, HALF, 256), F32),
            dma((8, 3)), dma((5,)),
            dma((21,)), dma((21,)),
            dma((8,)), dma((8,)),
            dma((6,)), dma((6,)),
            dma((4,)), dma((4,)),
            dma((4, 2)), dma((4, 2)),
            dma((4, 2)), dma((4, 2)),
            dma((4, 2)), dma((4, 2)),
            dma((4, 2)), dma((4, 2)),
        ],
        compiler_params=pltpu.CompilerParams(
            collective_id=0, has_side_effects=True, vmem_limit_bytes=60 * 2**20
        ),
        name="star_query",
    )(
        hidden, norm_gain.reshape(64, 128), w_query, w_key, w_value,
        cache_keys, cache_values, cache_lengths, tables,
    )


def solution(mesh):
    placed = (
        P("ctx", "tensor"),
        P(),
        P(None, "tensor"),
        P(None, "tensor"),
        P(None, "tensor"),
        P("ctx", "tensor"),
        P("ctx", "tensor"),
        P("ctx"),
    )
    return jax.shard_map(
        local, mesh=mesh, in_specs=placed, out_specs=P("ctx", "tensor"), check_vma=False
    )
```

```python
import functools

import jax
import jax.numpy as jnp
import numpy as np
from jax import lax
from jax.experimental import pallas as pl
from jax.experimental.pallas import tpu as pltpu
from jax.sharding import PartitionSpec as P

HEAD_DIM = 128
ROWS = 128
FEAT = 1024
SLOTS = 1024
HEADS = 8
HALF = 4 * ROWS
TILE = 512
KEYS = 4 * SLOTS + 2 * TILE
WIDTH = HEADS * HEAD_DIM + 2 * HEAD_DIM
SCALE = 1.0 / HEAD_DIM**0.5
EXP2 = SCALE / float(np.log(2.0))
LOW = -1e30
MESH = pl.DeviceIdType.MESH
NT = (((1,), (1,)), ((), ()))
F32, BF16 = jnp.float32, jnp.bfloat16


def rotary_tables():
    half = HEAD_DIM // 2
    freq = 500000.0 ** (-2.0 * np.arange(half) / HEAD_DIM)
    angle = (16384 + np.arange(2048))[:, None] * freq[None, :]
    cosine, sine = np.cos(angle), np.sin(angle)
    both = np.stack(
        [np.concatenate([cosine, cosine], 1), np.concatenate([-sine, sine], 1)]
    )
    both = both.reshape(2, 16, ROWS, HEAD_DIM).transpose(1, 0, 2, 3)
    return both.astype(np.float32)


def eye():
    row = lax.broadcasted_iota(jnp.int32, (ROWS, ROWS), 0)
    col = lax.broadcasted_iota(jnp.int32, (ROWS, ROWS), 1)
    return row == col


def to_row(column):
    return jnp.sum(jnp.where(eye(), column, 0.0), axis=0, keepdims=True)


def to_column(row):
    wide = jnp.broadcast_to(row, (ROWS, ROWS))
    return jnp.sum(jnp.where(eye(), wide, 0.0), axis=1, keepdims=True)


def scores(q, keys):
    return lax.dot_general(q, keys, NT, preferred_element_type=F32)


def absorb(s, state, values, bias=None):
    if bias is not None:
        s = (s.reshape(4, ROWS, TILE) + bias[None]).reshape(HALF, TILE)
    top = jnp.max(s, axis=1, keepdims=True)
    if state is not None:
        top = jnp.maximum(state[0], top)
    p = jnp.exp2((s - top) * EXP2).astype(BF16)
    add = jnp.dot(p, values, preferred_element_type=F32)
    if state is None:
        return top, add
    return top, state[1] * jnp.exp2((state[0] - top) * EXP2) + add


def kernel(
    hid, gain, wq, wk, wv, ck, cv, lens, tab, out,
    w, hbuf, gbuf, tabv, ssq, rs, acc, kvraw, lensb, kp, vp, qbuf, pout, pin, lout, lin, mst, ost,
    wsem, lsem, hs, hr, ss, sr, ks, kr, ls, lr, os_, or_, qs, qr, ps, pr, es, er,
):
    ci, ti = lax.axis_index("ctx"), lax.axis_index("tensor")
    z, x = lax.div(ci, 4), lax.rem(ci, 4)
    y, c = lax.div(ti, 2), lax.rem(ti, 2)

    def at_y(d, other=False):
        core = 1 - c if other else c
        return 2 * lax.rem(y + d, 4) + core

    def at_x(d):
        return lax.rem(x + d, 4)

    def at_z(d):
        return lax.rem(z + d, 4)

    def x_dev(d):
        return (4 * z + at_x(d), ti)

    def z_dev(d):
        return (4 * at_z(d) + x, ti)

    def y_dev(d):
        return (ci, at_y(d))

    sib = (ci, at_y(0, True))
    sends = []

    def remote(src, dst, send_sem, recv_sem, device):
        return pltpu.make_async_remote_copy(
            src_ref=src, dst_ref=dst, send_sem=send_sem, recv_sem=recv_sem,
            device_id=device, device_id_type=MESH,
        )

    def send(*args):
        copy = remote(*args)
        copy.start()
        sends.append(copy)

    order = [at_y(0), at_y(0, True), at_y(3), at_y(1), at_y(3, True), at_y(1, True), at_y(2), at_y(2, True)]
    own_h = pltpu.make_async_copy(hid, hbuf.at[ti], lsem.at[0])
    own_h.start()
    load_gain = pltpu.make_async_copy(gain, gbuf, lsem.at[1])
    load_gain.start()

    barrier = pltpu.get_barrier_semaphore()
    peers = [(ci, lax.rem(ti + d, 8)) for d in range(1, 8)]
    peers += [x_dev(d) for d in (1, 2, 3)] + [z_dev(d) for d in (1, 2, 3)]
    for peer in peers:
        pl.semaphore_signal(barrier, inc=1, device_id=peer, device_id_type=MESH)

    w_loads = []
    for i, t in enumerate(order):
        rows = pl.ds(pl.multiple_of(t * FEAT, FEAT), FEAT)
        loads = [
            pltpu.make_async_copy(wq.at[rows], w.at[rows, pl.ds(0, FEAT)], wsem.at[i, 0]),
            pltpu.make_async_copy(wk.at[rows], w.at[rows, pl.ds(FEAT, 128)], wsem.at[i, 1]),
            pltpu.make_async_copy(wv.at[rows], w.at[rows, pl.ds(FEAT + 128, 128)], wsem.at[i, 2]),
        ]
        for load in loads:
            load.start()
        w_loads.append(loads)
    load_k = pltpu.make_async_copy(ck, kvraw.at[x, 0], lsem.at[2])
    load_k.start()
    load_v = pltpu.make_async_copy(cv, kvraw.at[x, 1], lsem.at[3])
    load_v.start()
    load_tab = pltpu.make_async_copy(tab.at[ci], tabv, lsem.at[4])
    load_tab.start()
    lensb[x] = jnp.full((8, 128), lens[0], jnp.int32)
    own_h.wait()
    wide = hbuf[ti].astype(F32)
    squares = jnp.sum(wide * wide, axis=1, keepdims=True)
    ssq[ti] = jnp.broadcast_to(to_row(jnp.broadcast_to(squares, (ROWS, ROWS))), (8, 128))

    pl.semaphore_wait(barrier, len(peers))

    def h_ref(t, first, count):
        return hbuf.at[t, :, pl.ds(256 * first, 256 * count)]

    def h_send(i, t, first, count, device):
        send(h_ref(t, first, count), h_ref(t, first, count), hs.at[i], hr.at[i], device)

    def h_wait(i, t, first, count):
        ref = h_ref(t, first, count)
        remote(ref, ref, hs.at[i], hr.at[i], sib).wait_recv()

    for d in range(1, 8):
        send(ssq.at[ti], ssq.at[ti], ss.at[d], sr.at[d], (ci, lax.rem(ti + d, 8)))
    for k in range(4):
        h_send(k, ti, k, 1, y_dev(1))
        h_send(4 + k, ti, (k + 2) % 4, 1, y_dev(3))
        if k == 0:
            h_send(12, ti, 0, 4, sib)
    for d in (1, 2, 3):
        send(lensb.at[x], lensb.at[x], ls.at[d], lr.at[d], x_dev(d))
    send(ck, kvraw.at[x, 0], ks.at[0], kr.at[0], x_dev(1))
    send(cv, kvraw.at[x, 1], ks.at[1], kr.at[1], x_dev(3))
    send(cv, kvraw.at[x, 1], ks.at[2], kr.at[2], x_dev(1))
    send(ck, kvraw.at[x, 0], ks.at[3], kr.at[3], x_dev(3))

    def kv_wait(i, d, which):
        ref = kvraw.at[at_x(d), which]
        remote(ref, ref, ks.at[i], kr.at[i], sib).wait_recv()

    def kv_pass(i, d, which, device):
        ref = kvraw.at[at_x(d), which]
        send(ref, ref, ks.at[i], kr.at[i], device)

    load_gain.wait()
    for d in range(1, 8):
        ref = ssq.at[lax.rem(ti + 8 - d, 8)]
        remote(ref, ref, ss.at[d], sr.at[d], sib).wait_recv()
    total = jnp.sum(ssq[...], axis=0)
    inverse = lax.rsqrt(total * (1.0 / 8192.0) + 1e-5)
    rs[...] = jnp.broadcast_to(to_column(inverse[0:1, :]), (ROWS, ROWS))

    places = {0: 0, 3: 1, 1: 2, 2: 3}

    def slots(d):
        return slice(places[d] * SLOTS, (places[d] + 1) * SLOTS)

    def mark(d):
        row = lax.broadcasted_iota(jnp.int32, (SLOTS, 128), 0)
        valid = row < lensb[at_x(d)][0:1, :]
        vp[slots(d), 128:256] = jnp.where(valid, 1.0, 0.0).astype(BF16)

    def prepare(d):
        xi = at_x(d)
        valid = vp[slots(d), 128:256]
        first = jnp.broadcast_to(kvraw[xi, 0, 0:16, :].astype(F32)[0:1, :], (SLOTS, 128)).astype(BF16)
        kp[slots(d), :] = kvraw[xi, 0] * valid + first * (1 - valid)
        vp[slots(d), 0:128] = kvraw[xi, 1] * valid

    def project(i, first=0, count=4):
        t = order[i]
        g = gbuf[pl.ds(pl.multiple_of(t * 8, 8), 8), :]
        pieces = []
        for k in range(2 * first, 2 * (first + count)):
            piece = hbuf[t, :, k * 128 : (k + 1) * 128].astype(F32)
            pieces.append((piece * rs[...] * g[k : k + 1, :]).astype(BF16))
        normed = jnp.concatenate(pieces, axis=1)
        rows = pl.ds(pl.multiple_of(t * FEAT + first * 256, 256), count * 256)
        return jnp.dot(normed, w[rows, :], preferred_element_type=F32)

    def loaded(*chunks):
        for i in chunks:
            for load in w_loads[i]:
                load.wait()

    left, right, far = at_y(3), at_y(1), at_y(2)
    loaded(0, 1)
    acc[...] = project(0)
    h_wait(12, order[1], 0, 4)
    acc[...] += project(1)
    for d in (1, 2, 3):
        ref = lensb.at[at_x(4 - d)]
        remote(ref, ref, ls.at[d], lr.at[d], sib).wait_recv()
    for d in range(4):
        mark(d)
    for k in (0, 1):
        h_wait(k, left, k, 1)
        h_send(8 + k, left, k, 1, y_dev(1))
        h_wait(4 + k, right, 2 + k, 1)
        h_send(10 + k, right, 2 + k, 1, y_dev(3))
    h_send(13, left, 0, 2, sib)
    h_send(14, right, 2, 2, sib)
    loaded(2, 3)
    acc[...] += project(2, 0, 2) + project(3, 2, 2)
    h_wait(13, order[4], 0, 2)
    h_wait(14, order[5], 2, 2)
    loaded(4, 5)
    acc[...] += project(4, 0, 2) + project(5, 2, 2)
    for k in (2, 3):
        h_wait(k, left, k, 1)
        h_wait(4 + k, right, k - 2, 1)
    h_send(15, left, 2, 2, sib)
    h_send(16, right, 0, 2, sib)
    acc[...] += project(2, 2, 2) + project(3, 0, 2)
    h_wait(15, order[4], 2, 2)
    h_wait(16, order[5], 0, 2)
    acc[...] += project(4, 2, 2) + project(5, 0, 2)
    h_wait(8, far, 0, 1)
    h_send(17, far, 0, 1, sib)
    h_wait(10, far, 2, 1)
    h_send(18, far, 2, 1, sib)
    loaded(6, 7)
    acc[...] += project(6, 0, 1) + project(6, 2, 1)
    load_k.wait()
    load_v.wait()
    prepare(0)
    vp[4 * SLOTS : 4 * SLOTS + TILE, 128:256] = jnp.ones((TILE, 128), BF16)
    vp[4 * SLOTS + TILE :, :] = jnp.zeros((TILE, 256), BF16)
    kp[4 * SLOTS + TILE :, :] = jnp.broadcast_to(kvraw[x, 0, 0:16, :].astype(F32)[0:1, :], (TILE, 128)).astype(BF16)
    load_tab.wait()
    h_wait(9, far, 1, 1)
    h_send(19, far, 1, 1, sib)
    h_wait(11, far, 3, 1)
    h_send(20, far, 3, 1, sib)
    h_wait(17, order[7], 0, 1)
    h_wait(18, order[7], 2, 1)
    acc[...] += project(6, 1, 1) + project(6, 3, 1) + project(7, 0, 1) + project(7, 2, 1)
    h_wait(19, order[7], 1, 1)
    h_wait(20, order[7], 3, 1)
    acc[...] += project(7, 1, 1) + project(7, 3, 1)

    def rotate(piece):
        return (piece * tabv[0] + pltpu.roll(piece, 64, 1) * tabv[1]).astype(BF16)

    own_rows = pl.ds(pl.multiple_of(4 * SLOTS + x * ROWS, ROWS), ROWS)
    kp[own_rows, :] = rotate(acc[:, FEAT : FEAT + 128])
    vp[own_rows, 0:128] = acc[:, FEAT + 128 :].astype(BF16)
    for d in (1, 3, 2):
        rows = kp.at[own_rows]
        send(rows, rows, os_.at[d, 0], or_.at[d, 0], x_dev(d))
        rows = vp.at[own_rows, pl.ds(0, 128)]
        send(rows, rows, os_.at[d, 1], or_.at[d, 1], x_dev(d))

    def q_send(d, half):
        send(qbuf.at[z, half], qbuf.at[z, half], qs.at[d, half], qr.at[d, half], z_dev(d))

    for h in range(HEADS):
        qbuf[z, h // 4, (h % 4) * 128 : (h % 4 + 1) * 128, :] = rotate(acc[:, h * 128 : (h + 1) * 128])
        if h == 3:
            q_send(1, 0)
            q_send(3, 0)

    def own_bias():
        row = lax.broadcasted_iota(jnp.int32, (ROWS, TILE), 0)
        col = lax.broadcasted_iota(jnp.int32, (ROWS, TILE), 1)
        return jnp.where(row - col >= -128 * x, 0.0, LOW)

    def finish(state, zi, half):
        top, both = state
        denominator = both[:, 128:]
        pout[zi, half] = (both[:, :128] / denominator).astype(BF16)
        tops = jnp.broadcast_to(top, (HALF, 128))
        parts = [slice(h * 128, (h + 1) * 128) for h in range(4)]
        top_rows = jnp.concatenate([to_row(tops[part]) for part in parts] * 2, axis=0)
        sum_rows = jnp.concatenate([to_row(denominator[part]) for part in parts] * 2, axis=0)
        lout[zi, half] = top_rows * SCALE + jnp.log(sum_rows)

    def run(*units):
        steps = [(unit, tile) for unit in units for tile in unit[2]]

        def rows(tile):
            return slice(tile * TILE, (tile + 1) * TILE) if isinstance(tile, int) else tile

        def ahead(step):
            unit, tile = step
            return scores(unit[0], kp[rows(tile), :])

        s = ahead(steps[0])
        state = None
        for n, (unit, tile) in enumerate(steps):
            later = ahead(steps[n + 1]) if n + 1 < len(steps) else None
            if n == 0 or steps[n - 1][0] is not unit:
                state = unit[1]
            state = absorb(s, state, vp[rows(tile), :], own_bias() if tile == 8 else None)
            s = later
            if n + 1 == len(steps) or steps[n + 1][0] is not unit:
                unit[3](state)

    def keep(half, state):
        mst[half] = jnp.broadcast_to(state[0], (HALF, 128))
        ost[half] = state[1]

    def kept(half):
        return mst[half][:, 0:1], ost[half]

    q_send(2, 0)
    q_send(2, 1)
    kv_wait(0, 3, 0)
    kv_pass(4, 3, 0, x_dev(1))
    kv_wait(1, 1, 1)
    kv_pass(5, 1, 1, x_dev(3))
    kv_wait(2, 3, 1)
    prepare(3)
    kv_wait(3, 1, 0)
    prepare(1)
    run(
        (qbuf[z, 0], None, range(6), functools.partial(keep, 0)),
        (qbuf[z, 1], None, range(6), functools.partial(keep, 1)),
    )
    q_send(1, 1)
    q_send(3, 1)

    def back(d, half):
        zi = at_z(d)
        return [
            remote(pout.at[zi, half], pin.at[z, half], ps.at[d, half], pr.at[d, half], z_dev(d)),
            remote(lout.at[zi, half], lin.at[z, half], es.at[d, half], er.at[d, half], z_dev(d)),
        ]

    def end(d, half, *returns):
        def call(state):
            finish(state, at_z(d), half)
            for which in returns:
                for copy in back(*which):
                    copy.start()

        return call

    def q_wait(d, half):
        ref = qbuf.at[at_z(d), half]
        remote(ref, ref, qs.at[4 - d, half], qr.at[4 - d, half], sib).wait_recv()

    def last(d):
        return pl.ds(pl.multiple_of(4 * SLOTS + TILE * lax.div(z + d, 4), TILE), TILE)

    def unit(d, half, *returns):
        return (qbuf[at_z(d), half], None, [*range(8), last(d)], end(d, half, *returns))

    q_wait(1, 0)
    q_wait(3, 0)
    run(
        (qbuf[at_z(1), 0], None, range(6), functools.partial(keep, 2)),
        (qbuf[at_z(3), 0], None, range(6), functools.partial(keep, 3)),
    )
    kv_wait(4, 2, 0)
    kv_wait(5, 2, 1)
    prepare(2)
    for d in (1, 2, 3):
        rows = pl.ds(pl.multiple_of(4 * SLOTS + at_x(4 - d) * ROWS, ROWS), ROWS)
        ref = kp.at[rows]
        remote(ref, ref, os_.at[d, 0], or_.at[d, 0], sib).wait_recv()
        ref = vp.at[rows, pl.ds(0, 128)]
        remote(ref, ref, os_.at[d, 1], or_.at[d, 1], sib).wait_recv()
    q_wait(2, 0)
    q_wait(2, 1)
    run(
        (qbuf[at_z(1), 0], kept(2), [6, 7, last(1)], end(1, 0)),
        (qbuf[at_z(3), 0], kept(3), [6, 7, last(3)], end(3, 0, (1, 0), (3, 0))),
        unit(2, 0),
        unit(2, 1, (2, 0), (2, 1)),
    )
    q_wait(1, 1)
    q_wait(3, 1)
    run(unit(1, 1), unit(3, 1, (1, 1), (3, 1)))

    def arrived(half):
        for d in (1, 2, 3):
            ref = pin.at[at_z(4 - d), half]
            remote(ref, ref, ps.at[d, half], pr.at[d, half], sib).wait_recv()
            ref = lin.at[at_z(4 - d), half]
            remote(ref, ref, es.at[d, half], er.at[d, half], sib).wait_recv()

    def combine(half):
        logs = [lout[z, half]] + [lin[at_z(d), half] for d in (1, 2, 3)]
        top = functools.reduce(jnp.maximum, logs)
        weights = [jnp.exp(log - top) for log in logs]
        denominator = functools.reduce(jnp.add, weights)
        weights = [weight / denominator for weight in weights]
        for h in range(4):
            rows = slice(h * 128, (h + 1) * 128)
            total = None
            for d in range(4):
                part = pout[z, half, rows, :] if d == 0 else pin[at_z(d), half, rows, :]
                term = part.astype(F32) * to_column(weights[d][h : h + 1, :])
                total = term if total is None else total + term
            head = half * 4 + h
            out[:, head * 128 : (head + 1) * 128] = total.astype(BF16)

    def end_first(state):
        finish(state, z, 0)
        combine(0)

    arrived(0)
    run(
        (qbuf[z, 0], kept(0), [6, 7, 8], end_first),
        (qbuf[z, 1], kept(1), [6, 7, 8], lambda state: finish(state, z, 1)),
    )
    arrived(1)
    combine(1)

    for copy in sends:
        copy.wait_send()
    for half in range(2):
        for d in (1, 2, 3):
            for copy in back(d, half):
                copy.wait_send()


def local(hidden, norm_gain, w_query, w_key, w_value, cache_keys, cache_values, cache_lengths):
    anywhere = pl.BlockSpec(memory_space=pl.ANY)
    tables = jnp.asarray(rotary_tables())
    dma = pltpu.SemaphoreType.DMA
    return pl.pallas_call(
        kernel,
        out_shape=jax.ShapeDtypeStruct((ROWS, FEAT), BF16),
        in_specs=[anywhere] * 7 + [pl.BlockSpec(memory_space=pltpu.SMEM), anywhere],
        out_specs=pl.BlockSpec(memory_space=pltpu.VMEM),
        scratch_shapes=[
            pltpu.VMEM((8 * FEAT, WIDTH), BF16),
            pltpu.VMEM((8, ROWS, FEAT), BF16),
            pltpu.VMEM((64, 128), F32),
            pltpu.VMEM((2, ROWS, 128), F32),
            pltpu.VMEM((8, 8, 128), F32),
            pltpu.VMEM((ROWS, ROWS), F32),
            pltpu.VMEM((ROWS, WIDTH), F32),
            pltpu.VMEM((4, 2, SLOTS, 128), BF16),
            pltpu.VMEM((4, 8, 128), jnp.int32),
            pltpu.VMEM((KEYS, 128), BF16),
            pltpu.VMEM((KEYS, 256), BF16),
            pltpu.VMEM((4, 2, HALF, 128), BF16),
            pltpu.VMEM((4, 2, HALF, 128), BF16),
            pltpu.VMEM((4, 2, HALF, 128), BF16),
            pltpu.VMEM((4, 2, 8, 128), F32),
            pltpu.VMEM((4, 2, 8, 128), F32),
            pltpu.VMEM((4, HALF, 128), F32),
            pltpu.VMEM((4, HALF, 256), F32),
            dma((8, 3)), dma((5,)),
            dma((21,)), dma((21,)),
            dma((8,)), dma((8,)),
            dma((6,)), dma((6,)),
            dma((4,)), dma((4,)),
            dma((4, 2)), dma((4, 2)),
            dma((4, 2)), dma((4, 2)),
            dma((4, 2)), dma((4, 2)),
            dma((4, 2)), dma((4, 2)),
        ],
        compiler_params=pltpu.CompilerParams(
            collective_id=0, has_side_effects=True, vmem_limit_bytes=60 * 2**20
        ),
        name="star_query",
    )(
        hidden, norm_gain.reshape(64, 128), w_query, w_key, w_value,
        cache_keys, cache_values, cache_lengths, tables,
    )


def solution(mesh):
    placed = (
        P("ctx", "tensor"),
        P(),
        P(None, "tensor"),
        P(None, "tensor"),
        P(None, "tensor"),
        P("ctx", "tensor"),
        P("ctx", "tensor"),
        P("ctx"),
    )
    return jax.shard_map(
        local, mesh=mesh, in_specs=placed, out_specs=P("ctx", "tensor"), check_vma=False
    )
```

```python
import functools

import jax
import jax.numpy as jnp
import numpy as np
from jax import lax
from jax.experimental import pallas as pl
from jax.experimental.pallas import tpu as pltpu
from jax.sharding import PartitionSpec as P

HEAD_DIM = 128
ROWS = 128
FEAT = 1024
SLOTS = 1024
HEADS = 8
HALF = 4 * ROWS
TILE = 512
KEYS = 4 * SLOTS + 2 * TILE
WIDTH = HEADS * HEAD_DIM + 2 * HEAD_DIM
SCALE = 1.0 / HEAD_DIM**0.5
EXP2 = SCALE / float(np.log(2.0))
LOW = -1e30
MESH = pl.DeviceIdType.MESH
NT = (((1,), (1,)), ((), ()))
F32, BF16 = jnp.float32, jnp.bfloat16


def rotary_tables():
    half = HEAD_DIM // 2
    freq = 500000.0 ** (-2.0 * np.arange(half) / HEAD_DIM)
    angle = (16384 + np.arange(2048))[:, None] * freq[None, :]
    cosine, sine = np.cos(angle), np.sin(angle)
    both = np.stack(
        [np.concatenate([cosine, cosine], 1), np.concatenate([-sine, sine], 1)]
    )
    both = both.reshape(2, 16, ROWS, HEAD_DIM).transpose(1, 0, 2, 3)
    return both.astype(np.float32)


def eye():
    row = lax.broadcasted_iota(jnp.int32, (ROWS, ROWS), 0)
    col = lax.broadcasted_iota(jnp.int32, (ROWS, ROWS), 1)
    return row == col


def to_row(column):
    return jnp.sum(jnp.where(eye(), column, 0.0), axis=0, keepdims=True)


def to_column(row):
    wide = jnp.broadcast_to(row, (ROWS, ROWS))
    return jnp.sum(jnp.where(eye(), wide, 0.0), axis=1, keepdims=True)


def scores(q, keys):
    return lax.dot_general(q, keys, NT, preferred_element_type=F32)


def absorb(s, state, values, bias=None):
    if bias is not None:
        s = (s.reshape(4, ROWS, TILE) + bias[None]).reshape(HALF, TILE)
    top = jnp.max(s, axis=1, keepdims=True)
    if state is not None:
        top = jnp.maximum(state[0], top)
    p = jnp.exp2((s - top) * EXP2).astype(BF16)
    add = jnp.dot(p, values, preferred_element_type=F32)
    if state is None:
        return top, add
    return top, state[1] * jnp.exp2((state[0] - top) * EXP2) + add


def kernel(
    hid, gain, wq, wk, wv, ck, cv, lens, tab, out,
    w, hbuf, gbuf, tabv, ssq, rs, acc, kvraw, lensb, kp, vp, qbuf, pout, pin, lout, lin, mst, ost,
    wsem, lsem, hs, hr, ss, sr, ks, kr, ls, lr, os_, or_, qs, qr, ps, pr, es, er,
):
    ci, ti = lax.axis_index("ctx"), lax.axis_index("tensor")
    z, x = lax.div(ci, 4), lax.rem(ci, 4)
    y, c = lax.div(ti, 2), lax.rem(ti, 2)

    def at_y(d, other=False):
        core = 1 - c if other else c
        return 2 * lax.rem(y + d, 4) + core

    def at_x(d):
        return lax.rem(x + d, 4)

    def at_z(d):
        return lax.rem(z + d, 4)

    def x_dev(d):
        return (4 * z + at_x(d), ti)

    def z_dev(d):
        return (4 * at_z(d) + x, ti)

    def y_dev(d):
        return (ci, at_y(d))

    sib = (ci, at_y(0, True))
    sends = []

    def remote(src, dst, send_sem, recv_sem, device):
        return pltpu.make_async_remote_copy(
            src_ref=src, dst_ref=dst, send_sem=send_sem, recv_sem=recv_sem,
            device_id=device, device_id_type=MESH,
        )

    def send(*args):
        copy = remote(*args)
        copy.start()
        sends.append(copy)

    order = [at_y(0), at_y(0, True), at_y(3), at_y(1), at_y(3, True), at_y(1, True), at_y(2), at_y(2, True)]
    own_h = pltpu.make_async_copy(hid, hbuf.at[ti], lsem.at[0])
    own_h.start()
    load_gain = pltpu.make_async_copy(gain, gbuf, lsem.at[1])
    load_gain.start()

    barrier = pltpu.get_barrier_semaphore()
    peers = [(ci, lax.rem(ti + d, 8)) for d in range(1, 8)]
    peers += [x_dev(d) for d in (1, 2, 3)] + [z_dev(d) for d in (1, 2, 3)]
    for peer in peers:
        pl.semaphore_signal(barrier, inc=1, device_id=peer, device_id_type=MESH)

    w_loads = []
    for i, t in enumerate(order):
        rows = pl.ds(pl.multiple_of(t * FEAT, FEAT), FEAT)
        loads = [
            pltpu.make_async_copy(wq.at[rows], w.at[rows, pl.ds(0, FEAT)], wsem.at[i, 0]),
            pltpu.make_async_copy(wk.at[rows], w.at[rows, pl.ds(FEAT, 128)], wsem.at[i, 1]),
            pltpu.make_async_copy(wv.at[rows], w.at[rows, pl.ds(FEAT + 128, 128)], wsem.at[i, 2]),
        ]
        for load in loads:
            load.start()
        w_loads.append(loads)
    load_k = pltpu.make_async_copy(ck, kvraw.at[x, 0], lsem.at[2])
    load_k.start()
    load_v = pltpu.make_async_copy(cv, kvraw.at[x, 1], lsem.at[3])
    load_v.start()
    load_tab = pltpu.make_async_copy(tab.at[ci], tabv, lsem.at[4])
    load_tab.start()
    lensb[x] = jnp.full((8, 128), lens[0], jnp.int32)
    own_h.wait()
    wide = hbuf[ti].astype(F32)
    squares = jnp.sum(wide * wide, axis=1, keepdims=True)
    ssq[ti] = jnp.broadcast_to(to_row(jnp.broadcast_to(squares, (ROWS, ROWS))), (8, 128))

    pl.semaphore_wait(barrier, len(peers))

    def h_ref(t, first, count):
        return hbuf.at[t, :, pl.ds(256 * first, 256 * count)]

    def h_send(i, t, first, count, device):
        send(h_ref(t, first, count), h_ref(t, first, count), hs.at[i], hr.at[i], device)

    def h_wait(i, t, first, count):
        ref = h_ref(t, first, count)
        remote(ref, ref, hs.at[i], hr.at[i], sib).wait_recv()

    for d in range(1, 8):
        send(ssq.at[ti], ssq.at[ti], ss.at[d], sr.at[d], (ci, lax.rem(ti + d, 8)))
    for k in range(4):
        h_send(k, ti, k, 1, y_dev(1))
        h_send(4 + k, ti, (k + 2) % 4, 1, y_dev(3))
        if k == 0:
            h_send(12, ti, 0, 4, sib)
    for d in (1, 2, 3):
        send(lensb.at[x], lensb.at[x], ls.at[d], lr.at[d], x_dev(d))
    send(ck, kvraw.at[x, 0], ks.at[0], kr.at[0], x_dev(1))
    send(cv, kvraw.at[x, 1], ks.at[1], kr.at[1], x_dev(3))
    send(cv, kvraw.at[x, 1], ks.at[2], kr.at[2], x_dev(1))
    send(ck, kvraw.at[x, 0], ks.at[3], kr.at[3], x_dev(3))

    def kv_wait(i, d, which):
        ref = kvraw.at[at_x(d), which]
        remote(ref, ref, ks.at[i], kr.at[i], sib).wait_recv()

    def kv_pass(i, d, which, device):
        ref = kvraw.at[at_x(d), which]
        send(ref, ref, ks.at[i], kr.at[i], device)

    load_gain.wait()
    for d in range(1, 8):
        ref = ssq.at[lax.rem(ti + 8 - d, 8)]
        remote(ref, ref, ss.at[d], sr.at[d], sib).wait_recv()
    total = jnp.sum(ssq[...], axis=0)
    inverse = lax.rsqrt(total * (1.0 / 8192.0) + 1e-5)
    rs[...] = jnp.broadcast_to(to_column(inverse[0:1, :]), (ROWS, ROWS))

    places = {0: 0, 3: 1, 1: 2, 2: 3}

    def slots(d):
        return slice(places[d] * SLOTS, (places[d] + 1) * SLOTS)

    def mark(d):
        row = lax.broadcasted_iota(jnp.int32, (SLOTS, 128), 0)
        valid = row < lensb[at_x(d)][0:1, :]
        vp[slots(d), 128:256] = jnp.where(valid, 1.0, 0.0).astype(BF16)

    def prepare(d):
        xi = at_x(d)
        valid = vp[slots(d), 128:256]
        first = jnp.broadcast_to(kvraw[xi, 0, 0:16, :].astype(F32)[0:1, :], (SLOTS, 128)).astype(BF16)
        kp[slots(d), :] = kvraw[xi, 0] * valid + first * (1 - valid)
        vp[slots(d), 0:128] = kvraw[xi, 1] * valid

    def project(i, first=0, count=4):
        t = order[i]
        g = gbuf[pl.ds(pl.multiple_of(t * 8, 8), 8), :]
        pieces = []
        for k in range(2 * first, 2 * (first + count)):
            piece = hbuf[t, :, k * 128 : (k + 1) * 128].astype(F32)
            pieces.append((piece * rs[...] * g[k : k + 1, :]).astype(BF16))
        normed = jnp.concatenate(pieces, axis=1)
        rows = pl.ds(pl.multiple_of(t * FEAT + first * 256, 256), count * 256)
        return jnp.dot(normed, w[rows, :], preferred_element_type=F32)

    def loaded(*chunks):
        for i in chunks:
            for load in w_loads[i]:
                load.wait()

    left, right, far = at_y(3), at_y(1), at_y(2)
    loaded(0, 1)
    acc[...] = project(0)
    h_wait(12, order[1], 0, 4)
    acc[...] += project(1)
    for k in (0, 1):
        h_wait(k, left, k, 1)
        h_send(8 + k, left, k, 1, y_dev(1))
        h_wait(4 + k, right, 2 + k, 1)
        h_send(10 + k, right, 2 + k, 1, y_dev(3))
    h_send(13, left, 0, 2, sib)
    h_send(14, right, 2, 2, sib)
    loaded(2, 3)
    acc[...] += project(2, 0, 2) + project(3, 2, 2)
    h_wait(13, order[4], 0, 2)
    h_wait(14, order[5], 2, 2)
    loaded(4, 5)
    acc[...] += project(4, 0, 2) + project(5, 2, 2)
    for k in (2, 3):
        h_wait(k, left, k, 1)
        h_wait(4 + k, right, k - 2, 1)
    h_send(15, left, 2, 2, sib)
    h_send(16, right, 0, 2, sib)
    acc[...] += project(2, 2, 2) + project(3, 0, 2)
    h_wait(15, order[4], 2, 2)
    h_wait(16, order[5], 0, 2)
    acc[...] += project(4, 2, 2) + project(5, 0, 2)
    h_wait(8, far, 0, 1)
    h_send(17, far, 0, 1, sib)
    h_wait(10, far, 2, 1)
    h_send(18, far, 2, 1, sib)
    loaded(6, 7)
    acc[...] += project(6, 0, 1) + project(6, 2, 1)
    for d in (1, 2, 3):
        ref = lensb.at[at_x(4 - d)]
        remote(ref, ref, ls.at[d], lr.at[d], sib).wait_recv()
    for d in range(4):
        mark(d)
    load_k.wait()
    load_v.wait()
    prepare(0)
    vp[4 * SLOTS : 4 * SLOTS + TILE, 128:256] = jnp.ones((TILE, 128), BF16)
    vp[4 * SLOTS + TILE :, :] = jnp.zeros((TILE, 256), BF16)
    kp[4 * SLOTS + TILE :, :] = jnp.broadcast_to(kvraw[x, 0, 0:16, :].astype(F32)[0:1, :], (TILE, 128)).astype(BF16)
    load_tab.wait()
    h_wait(9, far, 1, 1)
    h_send(19, far, 1, 1, sib)
    h_wait(11, far, 3, 1)
    h_send(20, far, 3, 1, sib)
    h_wait(17, order[7], 0, 1)
    h_wait(18, order[7], 2, 1)
    acc[...] += project(6, 1, 1) + project(6, 3, 1) + project(7, 0, 1) + project(7, 2, 1)
    h_wait(19, order[7], 1, 1)
    h_wait(20, order[7], 3, 1)
    acc[...] += project(7, 1, 1) + project(7, 3, 1)

    def rotate(piece):
        return (piece * tabv[0] + pltpu.roll(piece, 64, 1) * tabv[1]).astype(BF16)

    def q_send(d, half):
        send(qbuf.at[z, half], qbuf.at[z, half], qs.at[d, half], qr.at[d, half], z_dev(d))

    def q_store(h):
        qbuf[z, h // 4, (h % 4) * 128 : (h % 4 + 1) * 128, :] = rotate(acc[:, h * 128 : (h + 1) * 128])

    for h in range(4):
        q_store(h)
    q_send(1, 0)
    q_send(3, 0)
    own_rows = pl.ds(pl.multiple_of(4 * SLOTS + x * ROWS, ROWS), ROWS)
    kp[own_rows, :] = rotate(acc[:, FEAT : FEAT + 128])
    vp[own_rows, 0:128] = acc[:, FEAT + 128 :].astype(BF16)
    for d in (1, 3, 2):
        rows = kp.at[own_rows]
        send(rows, rows, os_.at[d, 0], or_.at[d, 0], x_dev(d))
        rows = vp.at[own_rows, pl.ds(0, 128)]
        send(rows, rows, os_.at[d, 1], or_.at[d, 1], x_dev(d))
    for h in range(4, 8):
        q_store(h)

    def own_bias():
        row = lax.broadcasted_iota(jnp.int32, (ROWS, TILE), 0)
        col = lax.broadcasted_iota(jnp.int32, (ROWS, TILE), 1)
        return jnp.where(row - col >= -128 * x, 0.0, LOW)

    def finish(state, zi, half):
        top, both = state
        denominator = both[:, 128:]
        pout[zi, half] = (both[:, :128] / denominator).astype(BF16)
        tops = jnp.broadcast_to(top, (HALF, 128))
        parts = [slice(h * 128, (h + 1) * 128) for h in range(4)]
        top_rows = jnp.concatenate([to_row(tops[part]) for part in parts] * 2, axis=0)
        sum_rows = jnp.concatenate([to_row(denominator[part]) for part in parts] * 2, axis=0)
        lout[zi, half] = top_rows * SCALE + jnp.log(sum_rows)

    def run(*units):
        steps = [(unit, tile) for unit in units for tile in unit[2]]

        def rows(tile):
            return slice(tile * TILE, (tile + 1) * TILE) if isinstance(tile, int) else tile

        queries = {}

        def ahead(step):
            unit, tile = step
            if id(unit) not in queries:
                queries[id(unit)] = unit[0]() if callable(unit[0]) else unit[0]
            return scores(queries[id(unit)], kp[rows(tile), :])

        s = ahead(steps[0])
        state = None
        for n, (unit, tile) in enumerate(steps):
            later = ahead(steps[n + 1]) if n + 1 < len(steps) else None
            if n == 0 or steps[n - 1][0] is not unit:
                state = unit[1]
            state = absorb(s, state, vp[rows(tile), :], own_bias() if tile == 8 else None)
            s = later
            if n + 1 == len(steps) or steps[n + 1][0] is not unit:
                unit[3](state)

    def keep(half, state):
        mst[half] = jnp.broadcast_to(state[0], (HALF, 128))
        ost[half] = state[1]

    def kept(half):
        return mst[half][:, 0:1], ost[half]

    kv_wait(0, 3, 0)
    kv_pass(4, 3, 0, x_dev(1))
    kv_wait(1, 1, 1)
    kv_pass(5, 1, 1, x_dev(3))
    kv_wait(2, 3, 1)
    prepare(3)
    kv_wait(3, 1, 0)
    prepare(1)
    run(
        (qbuf[z, 0], None, range(6), functools.partial(keep, 0)),
        (qbuf[z, 1], None, range(4), functools.partial(keep, 1)),
    )
    q_send(1, 1)
    q_send(3, 1)

    def back(d, half):
        zi = at_z(d)
        return [
            remote(pout.at[zi, half], pin.at[z, half], ps.at[d, half], pr.at[d, half], z_dev(d)),
            remote(lout.at[zi, half], lin.at[z, half], es.at[d, half], er.at[d, half], z_dev(d)),
        ]

    def end(d, half, *returns):
        def call(state):
            finish(state, at_z(d), half)
            for which in returns:
                for copy in back(*which):
                    copy.start()

        return call

    def q_wait(d, half):
        ref = qbuf.at[at_z(d), half]
        remote(ref, ref, qs.at[4 - d, half], qr.at[4 - d, half], sib).wait_recv()

    def q_pass(d, half, to):
        ref = qbuf.at[at_z(d), half]
        send(ref, ref, qs.at[2, half], qr.at[2, half], z_dev(to))

    def q_far(half):
        q_wait(2, half)
        return qbuf[at_z(2), half]

    def last(d):
        return pl.ds(pl.multiple_of(4 * SLOTS + TILE * lax.div(z + d, 4), TILE), TILE)

    def unit(d, half, *returns):
        return (qbuf[at_z(d), half], None, [*range(8), last(d)], end(d, half, *returns))

    q_wait(1, 0)
    q_wait(3, 0)
    q_pass(3, 0, 1)
    run(
        (qbuf[at_z(1), 0], None, range(6), functools.partial(keep, 2)),
        (qbuf[at_z(3), 0], None, range(6), functools.partial(keep, 3)),
    )
    q_wait(1, 1)
    q_pass(1, 1, 3)
    kv_wait(4, 2, 0)
    kv_wait(5, 2, 1)
    prepare(2)
    for d in (1, 2, 3):
        rows = pl.ds(pl.multiple_of(4 * SLOTS + at_x(4 - d) * ROWS, ROWS), ROWS)
        ref = kp.at[rows]
        remote(ref, ref, os_.at[d, 0], or_.at[d, 0], sib).wait_recv()
        ref = vp.at[rows, pl.ds(0, 128)]
        remote(ref, ref, os_.at[d, 1], or_.at[d, 1], sib).wait_recv()
    run(
        (qbuf[at_z(1), 0], kept(2), [6, 7, last(1)], end(1, 0)),
        (qbuf[at_z(3), 0], kept(3), [6, 7, last(3)], end(3, 0, (1, 0), (3, 0))),
        (functools.partial(q_far, 0), None, [*range(8), last(2)], end(2, 0)),
        (functools.partial(q_far, 1), None, [*range(8), last(2)], end(2, 1, (2, 0), (2, 1))),
    )
    q_wait(3, 1)
    run(unit(1, 1), unit(3, 1, (1, 1), (3, 1)))

    def arrived(half):
        for d in (1, 2, 3):
            ref = pin.at[at_z(4 - d), half]
            remote(ref, ref, ps.at[d, half], pr.at[d, half], sib).wait_recv()
            ref = lin.at[at_z(4 - d), half]
            remote(ref, ref, es.at[d, half], er.at[d, half], sib).wait_recv()

    def combine(half):
        logs = [lout[z, half]] + [lin[at_z(d), half] for d in (1, 2, 3)]
        top = functools.reduce(jnp.maximum, logs)
        weights = [jnp.exp(log - top) for log in logs]
        denominator = functools.reduce(jnp.add, weights)
        weights = [weight / denominator for weight in weights]
        for h in range(4):
            rows = slice(h * 128, (h + 1) * 128)
            total = None
            for d in range(4):
                part = pout[z, half, rows, :] if d == 0 else pin[at_z(d), half, rows, :]
                term = part.astype(F32) * to_column(weights[d][h : h + 1, :])
                total = term if total is None else total + term
            head = half * 4 + h
            out[:, head * 128 : (head + 1) * 128] = total.astype(BF16)

    def end_first(state):
        finish(state, z, 0)
        combine(0)

    arrived(0)
    run(
        (qbuf[z, 0], kept(0), [6, 7, 8], end_first),
        (qbuf[z, 1], kept(1), [4, 5, 6, 7, 8], lambda state: finish(state, z, 1)),
    )
    arrived(1)
    combine(1)

    for copy in sends:
        copy.wait_send()
    for half in range(2):
        for d in (1, 2, 3):
            for copy in back(d, half):
                copy.wait_send()


def local(hidden, norm_gain, w_query, w_key, w_value, cache_keys, cache_values, cache_lengths):
    anywhere = pl.BlockSpec(memory_space=pl.ANY)
    tables = jnp.asarray(rotary_tables())
    dma = pltpu.SemaphoreType.DMA
    return pl.pallas_call(
        kernel,
        out_shape=jax.ShapeDtypeStruct((ROWS, FEAT), BF16),
        in_specs=[anywhere] * 7 + [pl.BlockSpec(memory_space=pltpu.SMEM), anywhere],
        out_specs=pl.BlockSpec(memory_space=pltpu.VMEM),
        scratch_shapes=[
            pltpu.VMEM((8 * FEAT, WIDTH), BF16),
            pltpu.VMEM((8, ROWS, FEAT), BF16),
            pltpu.VMEM((64, 128), F32),
            pltpu.VMEM((2, ROWS, 128), F32),
            pltpu.VMEM((8, 8, 128), F32),
            pltpu.VMEM((ROWS, ROWS), F32),
            pltpu.VMEM((ROWS, WIDTH), F32),
            pltpu.VMEM((4, 2, SLOTS, 128), BF16),
            pltpu.VMEM((4, 8, 128), jnp.int32),
            pltpu.VMEM((KEYS, 128), BF16),
            pltpu.VMEM((KEYS, 256), BF16),
            pltpu.VMEM((4, 2, HALF, 128), BF16),
            pltpu.VMEM((4, 2, HALF, 128), BF16),
            pltpu.VMEM((4, 2, HALF, 128), BF16),
            pltpu.VMEM((4, 2, 8, 128), F32),
            pltpu.VMEM((4, 2, 8, 128), F32),
            pltpu.VMEM((4, HALF, 128), F32),
            pltpu.VMEM((4, HALF, 256), F32),
            dma((8, 3)), dma((5,)),
            dma((21,)), dma((21,)),
            dma((8,)), dma((8,)),
            dma((6,)), dma((6,)),
            dma((4,)), dma((4,)),
            dma((4, 2)), dma((4, 2)),
            dma((4, 2)), dma((4, 2)),
            dma((4, 2)), dma((4, 2)),
            dma((4, 2)), dma((4, 2)),
        ],
        compiler_params=pltpu.CompilerParams(
            collective_id=0, has_side_effects=True, vmem_limit_bytes=60 * 2**20
        ),
        name="star_query",
    )(
        hidden, norm_gain.reshape(64, 128), w_query, w_key, w_value,
        cache_keys, cache_values, cache_lengths, tables,
    )


def solution(mesh):
    placed = (
        P("ctx", "tensor"),
        P(),
        P(None, "tensor"),
        P(None, "tensor"),
        P(None, "tensor"),
        P("ctx", "tensor"),
        P("ctx", "tensor"),
        P("ctx"),
    )
    return jax.shard_map(
        local, mesh=mesh, in_specs=placed, out_specs=P("ctx", "tensor"), check_vma=False
    )
```

```python
import functools

import jax
import jax.numpy as jnp
import numpy as np
from jax import lax
from jax.experimental import pallas as pl
from jax.experimental.pallas import tpu as pltpu
from jax.sharding import PartitionSpec as P

HEAD_DIM = 128
ROWS = 128
FEAT = 1024
SLOTS = 1024
HEADS = 8
HALF = 4 * ROWS
TILE = 512
KEYS = 4 * SLOTS + 2 * TILE
WIDTH = HEADS * HEAD_DIM + 2 * HEAD_DIM
SCALE = 1.0 / HEAD_DIM**0.5
EXP2 = SCALE / float(np.log(2.0))
LOW = -1e30
MESH = pl.DeviceIdType.MESH
NT = (((1,), (1,)), ((), ()))
F32, BF16 = jnp.float32, jnp.bfloat16


def rotary_tables():
    half = HEAD_DIM // 2
    freq = 500000.0 ** (-2.0 * np.arange(half) / HEAD_DIM)
    angle = (16384 + np.arange(2048))[:, None] * freq[None, :]
    cosine, sine = np.cos(angle), np.sin(angle)
    both = np.stack(
        [np.concatenate([cosine, cosine], 1), np.concatenate([-sine, sine], 1)]
    )
    both = both.reshape(2, 16, ROWS, HEAD_DIM).transpose(1, 0, 2, 3)
    return both.astype(np.float32)


def eye():
    row = lax.broadcasted_iota(jnp.int32, (ROWS, ROWS), 0)
    col = lax.broadcasted_iota(jnp.int32, (ROWS, ROWS), 1)
    return row == col


def to_row(column):
    return jnp.sum(jnp.where(eye(), column, 0.0), axis=0, keepdims=True)


def to_column(row):
    wide = jnp.broadcast_to(row, (ROWS, ROWS))
    return jnp.sum(jnp.where(eye(), wide, 0.0), axis=1, keepdims=True)


def scores(q, keys):
    return lax.dot_general(q, keys, NT, preferred_element_type=F32)


def absorb(s, state, values, bias=None):
    if bias is not None:
        s = (s.reshape(4, ROWS, TILE) + bias[None]).reshape(HALF, TILE)
    top = jnp.max(s, axis=1, keepdims=True)
    if state is not None:
        top = jnp.maximum(state[0], top)
    p = jnp.exp2((s - top) * EXP2).astype(BF16)
    add = jnp.dot(p, values, preferred_element_type=F32)
    if state is None:
        return top, add
    return top, state[1] * jnp.exp2((state[0] - top) * EXP2) + add


def kernel(
    hid, gain, wq, wk, wv, ck, cv, lens, tab, out,
    w, hbuf, gbuf, tabv, ssq, rs, acc, kvraw, lensb, kp, vp, qbuf, pout, pin, lout, lin, mst, ost,
    wsem, lsem, hs, hr, ss, sr, ks, kr, ls, lr, os_, or_, qs, qr, ps, pr, es, er,
):
    ci, ti = lax.axis_index("ctx"), lax.axis_index("tensor")
    z, x = lax.div(ci, 4), lax.rem(ci, 4)
    y, c = lax.div(ti, 2), lax.rem(ti, 2)

    def at_y(d, other=False):
        core = 1 - c if other else c
        return 2 * lax.rem(y + d, 4) + core

    def at_x(d):
        return lax.rem(x + d, 4)

    def at_z(d):
        return lax.rem(z + d, 4)

    def x_dev(d):
        return (4 * z + at_x(d), ti)

    def z_dev(d):
        return (4 * at_z(d) + x, ti)

    def y_dev(d):
        return (ci, at_y(d))

    sib = (ci, at_y(0, True))
    sends = []

    def remote(src, dst, send_sem, recv_sem, device):
        return pltpu.make_async_remote_copy(
            src_ref=src, dst_ref=dst, send_sem=send_sem, recv_sem=recv_sem,
            device_id=device, device_id_type=MESH,
        )

    def send(*args):
        copy = remote(*args)
        copy.start()
        sends.append(copy)

    order = [at_y(0), at_y(0, True), at_y(3), at_y(1), at_y(3, True), at_y(1, True), at_y(2), at_y(2, True)]
    own_h = pltpu.make_async_copy(hid, hbuf.at[ti], lsem.at[0])
    own_h.start()
    load_gain = pltpu.make_async_copy(gain, gbuf, lsem.at[1])
    load_gain.start()

    barrier = pltpu.get_barrier_semaphore()
    peers = [(ci, lax.rem(ti + d, 8)) for d in range(1, 8)]
    peers += [x_dev(d) for d in (1, 2, 3)] + [z_dev(d) for d in (1, 2, 3)]
    for peer in peers:
        pl.semaphore_signal(barrier, inc=1, device_id=peer, device_id_type=MESH)

    w_loads = []
    for i, t in enumerate(order):
        rows = pl.ds(pl.multiple_of(t * FEAT, FEAT), FEAT)
        loads = [
            pltpu.make_async_copy(wq.at[rows], w.at[rows, pl.ds(0, FEAT)], wsem.at[i, 0]),
            pltpu.make_async_copy(wk.at[rows], w.at[rows, pl.ds(FEAT, 128)], wsem.at[i, 1]),
            pltpu.make_async_copy(wv.at[rows], w.at[rows, pl.ds(FEAT + 128, 128)], wsem.at[i, 2]),
        ]
        for load in loads:
            load.start()
        w_loads.append(loads)
    load_k = pltpu.make_async_copy(ck, kvraw.at[x, 0], lsem.at[2])
    load_k.start()
    load_v = pltpu.make_async_copy(cv, kvraw.at[x, 1], lsem.at[3])
    load_v.start()
    load_tab = pltpu.make_async_copy(tab.at[ci], tabv, lsem.at[4])
    load_tab.start()
    lensb[x] = jnp.full((8, 128), lens[0], jnp.int32)
    own_h.wait()
    wide = hbuf[ti].astype(F32)
    squares = jnp.sum(wide * wide, axis=1, keepdims=True)
    ssq[ti] = jnp.broadcast_to(to_row(jnp.broadcast_to(squares, (ROWS, ROWS))), (8, 128))

    pl.semaphore_wait(barrier, len(peers))

    def h_ref(t, first, count):
        return hbuf.at[t, :, pl.ds(256 * first, 256 * count)]

    def h_send(i, t, first, count, device):
        send(h_ref(t, first, count), h_ref(t, first, count), hs.at[i], hr.at[i], device)

    def h_wait(i, t, first, count):
        ref = h_ref(t, first, count)
        remote(ref, ref, hs.at[i], hr.at[i], sib).wait_recv()

    for d in range(1, 8):
        send(ssq.at[ti], ssq.at[ti], ss.at[d], sr.at[d], (ci, lax.rem(ti + d, 8)))
    for k in range(4):
        h_send(k, ti, k, 1, y_dev(1))
        h_send(4 + k, ti, (k + 2) % 4, 1, y_dev(3))
        if k == 0:
            h_send(12, ti, 0, 4, sib)
    for d in (1, 2, 3):
        send(lensb.at[x], lensb.at[x], ls.at[d], lr.at[d], x_dev(d))
    send(ck, kvraw.at[x, 0], ks.at[0], kr.at[0], x_dev(1))
    send(cv, kvraw.at[x, 1], ks.at[1], kr.at[1], x_dev(3))
    send(cv, kvraw.at[x, 1], ks.at[2], kr.at[2], x_dev(1))
    send(ck, kvraw.at[x, 0], ks.at[3], kr.at[3], x_dev(3))

    def kv_wait(i, d, which):
        ref = kvraw.at[at_x(d), which]
        remote(ref, ref, ks.at[i], kr.at[i], sib).wait_recv()

    def kv_pass(i, d, which, device):
        ref = kvraw.at[at_x(d), which]
        send(ref, ref, ks.at[i], kr.at[i], device)

    load_gain.wait()
    for d in range(1, 8):
        ref = ssq.at[lax.rem(ti + 8 - d, 8)]
        remote(ref, ref, ss.at[d], sr.at[d], sib).wait_recv()
    total = jnp.sum(ssq[...], axis=0)
    inverse = lax.rsqrt(total * (1.0 / 8192.0) + 1e-5)
    rs[...] = jnp.broadcast_to(to_column(inverse[0:1, :]), (ROWS, ROWS))

    places = {0: 0, 3: 1, 1: 2, 2: 3}

    def slots(d):
        return slice(places[d] * SLOTS, (places[d] + 1) * SLOTS)

    def mark(d):
        row = lax.broadcasted_iota(jnp.int32, (SLOTS, 128), 0)
        valid = row < lensb[at_x(d)][0:1, :]
        vp[slots(d), 128:256] = jnp.where(valid, 1.0, 0.0).astype(BF16)

    def prepare(d):
        xi = at_x(d)
        valid = vp[slots(d), 128:256]
        first = jnp.broadcast_to(kvraw[xi, 0, 0:16, :].astype(F32)[0:1, :], (SLOTS, 128)).astype(BF16)
        kp[slots(d), :] = kvraw[xi, 0] * valid + first * (1 - valid)
        vp[slots(d), 0:128] = kvraw[xi, 1] * valid

    def project(i, first=0, count=4):
        t = order[i]
        g = gbuf[pl.ds(pl.multiple_of(t * 8, 8), 8), :]
        pieces = []
        for k in range(2 * first, 2 * (first + count)):
            piece = hbuf[t, :, k * 128 : (k + 1) * 128].astype(F32)
            pieces.append((piece * rs[...] * g[k : k + 1, :]).astype(BF16))
        normed = jnp.concatenate(pieces, axis=1)
        rows = pl.ds(pl.multiple_of(t * FEAT + first * 256, 256), count * 256)
        return jnp.dot(normed, w[rows, :], preferred_element_type=F32)

    def loaded(*chunks):
        for i in chunks:
            for load in w_loads[i]:
                load.wait()

    left, right, far = at_y(3), at_y(1), at_y(2)
    loaded(0, 1)
    acc[...] = project(0)
    h_wait(12, order[1], 0, 4)
    acc[...] += project(1)
    for k in (0, 1):
        h_wait(k, left, k, 1)
        h_send(8 + k, left, k, 1, y_dev(1))
        h_wait(4 + k, right, 2 + k, 1)
        h_send(10 + k, right, 2 + k, 1, y_dev(3))
    h_send(13, left, 0, 2, sib)
    h_send(14, right, 2, 2, sib)
    loaded(2, 3)
    acc[...] += project(2, 0, 2) + project(3, 2, 2)
    h_wait(13, order[4], 0, 2)
    h_wait(14, order[5], 2, 2)
    loaded(4, 5)
    acc[...] += project(4, 0, 2) + project(5, 2, 2)
    for k in (2, 3):
        h_wait(k, left, k, 1)
        h_wait(4 + k, right, k - 2, 1)
    h_send(15, left, 2, 2, sib)
    h_send(16, right, 0, 2, sib)
    acc[...] += project(2, 2, 2) + project(3, 0, 2)
    h_wait(15, order[4], 2, 2)
    h_wait(16, order[5], 0, 2)
    acc[...] += project(4, 2, 2) + project(5, 0, 2)
    h_wait(8, far, 0, 1)
    h_send(17, far, 0, 1, sib)
    h_wait(10, far, 2, 1)
    h_send(18, far, 2, 1, sib)
    loaded(6, 7)
    acc[...] += project(6, 0, 1) + project(6, 2, 1)
    for d in (1, 2, 3):
        ref = lensb.at[at_x(4 - d)]
        remote(ref, ref, ls.at[d], lr.at[d], sib).wait_recv()
    for d in range(4):
        mark(d)
    load_k.wait()
    load_v.wait()
    prepare(0)
    vp[4 * SLOTS : 4 * SLOTS + TILE, 128:256] = jnp.ones((TILE, 128), BF16)
    vp[4 * SLOTS + TILE :, :] = jnp.zeros((TILE, 256), BF16)
    kp[4 * SLOTS + TILE :, :] = jnp.broadcast_to(kvraw[x, 0, 0:16, :].astype(F32)[0:1, :], (TILE, 128)).astype(BF16)
    load_tab.wait()
    h_wait(9, far, 1, 1)
    h_send(19, far, 1, 1, sib)
    h_wait(11, far, 3, 1)
    h_send(20, far, 3, 1, sib)
    h_wait(17, order[7], 0, 1)
    h_wait(18, order[7], 2, 1)
    acc[...] += project(6, 1, 1) + project(6, 3, 1) + project(7, 0, 1) + project(7, 2, 1)
    h_wait(19, order[7], 1, 1)
    h_wait(20, order[7], 3, 1)
    acc[...] += project(7, 1, 1) + project(7, 3, 1)

    def rotate(piece):
        return (piece * tabv[0] + pltpu.roll(piece, 64, 1) * tabv[1]).astype(BF16)

    def q_send(d, half):
        send(qbuf.at[z, half], qbuf.at[z, half], qs.at[d, half], qr.at[d, half], z_dev(d))

    def q_store(h):
        qbuf[z, h // 4, (h % 4) * 128 : (h % 4 + 1) * 128, :] = rotate(acc[:, h * 128 : (h + 1) * 128])

    for half in range(2):
        for h in range(4 * half, 4 * half + 4):
            q_store(h)
        q_send(1, half)
        q_send(3, half)
    own_rows = pl.ds(pl.multiple_of(4 * SLOTS + x * ROWS, ROWS), ROWS)
    kp[own_rows, :] = rotate(acc[:, FEAT : FEAT + 128])
    vp[own_rows, 0:128] = acc[:, FEAT + 128 :].astype(BF16)
    for d in (1, 3, 2):
        rows = kp.at[own_rows]
        send(rows, rows, os_.at[d, 0], or_.at[d, 0], x_dev(d))
        rows = vp.at[own_rows, pl.ds(0, 128)]
        send(rows, rows, os_.at[d, 1], or_.at[d, 1], x_dev(d))

    def own_bias():
        row = lax.broadcasted_iota(jnp.int32, (ROWS, TILE), 0)
        col = lax.broadcasted_iota(jnp.int32, (ROWS, TILE), 1)
        return jnp.where(row - col >= -128 * x, 0.0, LOW)

    def finish(state, zi, half):
        top, both = state
        denominator = both[:, 128:]
        pout[zi, half] = (both[:, :128] / denominator).astype(BF16)
        tops = jnp.broadcast_to(top, (HALF, 128))
        parts = [slice(h * 128, (h + 1) * 128) for h in range(4)]
        top_rows = jnp.concatenate([to_row(tops[part]) for part in parts] * 2, axis=0)
        sum_rows = jnp.concatenate([to_row(denominator[part]) for part in parts] * 2, axis=0)
        lout[zi, half] = top_rows * SCALE + jnp.log(sum_rows)

    def run(*units):
        steps = [(unit, tile) for unit in units for tile in unit[2]]

        def rows(tile):
            return slice(tile * TILE, (tile + 1) * TILE) if isinstance(tile, int) else tile

        def ahead(step):
            unit, tile = step
            return scores(unit[0], kp[rows(tile), :])

        s = ahead(steps[0])
        state = None
        for n, (unit, tile) in enumerate(steps):
            later = ahead(steps[n + 1]) if n + 1 < len(steps) else None
            if n == 0 or steps[n - 1][0] is not unit:
                state = unit[1]
            state = absorb(s, state, vp[rows(tile), :], own_bias() if tile == 8 else None)
            s = later
            if n + 1 == len(steps) or steps[n + 1][0] is not unit:
                unit[3](state)

    def keep(half, state):
        mst[half] = jnp.broadcast_to(state[0], (HALF, 128))
        ost[half] = state[1]

    def kept(half):
        return mst[half][:, 0:1], ost[half]

    kv_wait(0, 3, 0)
    kv_pass(4, 3, 0, x_dev(1))
    kv_wait(1, 1, 1)
    kv_pass(5, 1, 1, x_dev(3))
    kv_wait(2, 3, 1)
    prepare(3)
    kv_wait(3, 1, 0)
    prepare(1)
    run(
        (qbuf[z, 0], None, range(6), functools.partial(keep, 0)),
        (qbuf[z, 1], None, range(6), functools.partial(keep, 1)),
    )

    def back(d, half):
        zi = at_z(d)
        return [
            remote(pout.at[zi, half], pin.at[z, half], ps.at[d, half], pr.at[d, half], z_dev(d)),
            remote(lout.at[zi, half], lin.at[z, half], es.at[d, half], er.at[d, half], z_dev(d)),
        ]

    def end(d, half, *returns):
        def call(state):
            finish(state, at_z(d), half)
            for which in returns:
                for copy in back(*which):
                    copy.start()

        return call

    def q_wait(d, half):
        ref = qbuf.at[at_z(d), half]
        remote(ref, ref, qs.at[4 - d, half], qr.at[4 - d, half], sib).wait_recv()

    def q_pass(d, half, to):
        ref = qbuf.at[at_z(d), half]
        send(ref, ref, qs.at[2, half], qr.at[2, half], z_dev(to))

    def last(d):
        return pl.ds(pl.multiple_of(4 * SLOTS + TILE * lax.div(z + d, 4), TILE), TILE)

    def unit(d, half, *returns):
        return (qbuf[at_z(d), half], None, [*range(8), last(d)], end(d, half, *returns))

    q_wait(1, 0)
    q_wait(3, 0)
    q_pass(3, 0, 1)
    q_wait(1, 1)
    q_pass(1, 1, 3)
    run(
        (qbuf[at_z(1), 0], None, range(6), functools.partial(keep, 2)),
        (qbuf[at_z(3), 0], None, range(6), functools.partial(keep, 3)),
    )
    kv_wait(4, 2, 0)
    kv_wait(5, 2, 1)
    prepare(2)
    for d in (1, 2, 3):
        rows = pl.ds(pl.multiple_of(4 * SLOTS + at_x(4 - d) * ROWS, ROWS), ROWS)
        ref = kp.at[rows]
        remote(ref, ref, os_.at[d, 0], or_.at[d, 0], sib).wait_recv()
        ref = vp.at[rows, pl.ds(0, 128)]
        remote(ref, ref, os_.at[d, 1], or_.at[d, 1], sib).wait_recv()
    q_wait(2, 0)
    q_wait(2, 1)
    run(
        (qbuf[at_z(1), 0], kept(2), [6, 7, last(1)], end(1, 0, (1, 0))),
        (qbuf[at_z(3), 0], kept(3), [6, 7, last(3)], end(3, 0, (3, 0))),
        unit(2, 0, (2, 0)),
        unit(2, 1, (2, 1)),
    )
    q_wait(3, 1)
    run(unit(1, 1, (1, 1)), unit(3, 1, (3, 1)))

    def arrived(half):
        for d in (1, 2, 3):
            ref = pin.at[at_z(4 - d), half]
            remote(ref, ref, ps.at[d, half], pr.at[d, half], sib).wait_recv()
            ref = lin.at[at_z(4 - d), half]
            remote(ref, ref, es.at[d, half], er.at[d, half], sib).wait_recv()

    def combine(half):
        logs = [lout[z, half]] + [lin[at_z(d), half] for d in (1, 2, 3)]
        top = functools.reduce(jnp.maximum, logs)
        weights = [jnp.exp(log - top) for log in logs]
        denominator = functools.reduce(jnp.add, weights)
        weights = [weight / denominator for weight in weights]
        for h in range(4):
            rows = slice(h * 128, (h + 1) * 128)
            total = None
            for d in range(4):
                part = pout[z, half, rows, :] if d == 0 else pin[at_z(d), half, rows, :]
                term = part.astype(F32) * to_column(weights[d][h : h + 1, :])
                total = term if total is None else total + term
            head = half * 4 + h
            out[:, head * 128 : (head + 1) * 128] = total.astype(BF16)

    def end_first(state):
        finish(state, z, 0)
        combine(0)

    arrived(0)
    run(
        (qbuf[z, 0], kept(0), [6, 7, 8], end_first),
        (qbuf[z, 1], kept(1), [6, 7, 8], lambda state: finish(state, z, 1)),
    )
    arrived(1)
    combine(1)

    for copy in sends:
        copy.wait_send()
    for half in range(2):
        for d in (1, 2, 3):
            for copy in back(d, half):
                copy.wait_send()


def local(hidden, norm_gain, w_query, w_key, w_value, cache_keys, cache_values, cache_lengths):
    anywhere = pl.BlockSpec(memory_space=pl.ANY)
    tables = jnp.asarray(rotary_tables())
    dma = pltpu.SemaphoreType.DMA
    return pl.pallas_call(
        kernel,
        out_shape=jax.ShapeDtypeStruct((ROWS, FEAT), BF16),
        in_specs=[anywhere] * 7 + [pl.BlockSpec(memory_space=pltpu.SMEM), anywhere],
        out_specs=pl.BlockSpec(memory_space=pltpu.VMEM),
        scratch_shapes=[
            pltpu.VMEM((8 * FEAT, WIDTH), BF16),
            pltpu.VMEM((8, ROWS, FEAT), BF16),
            pltpu.VMEM((64, 128), F32),
            pltpu.VMEM((2, ROWS, 128), F32),
            pltpu.VMEM((8, 8, 128), F32),
            pltpu.VMEM((ROWS, ROWS), F32),
            pltpu.VMEM((ROWS, WIDTH), F32),
            pltpu.VMEM((4, 2, SLOTS, 128), BF16),
            pltpu.VMEM((4, 8, 128), jnp.int32),
            pltpu.VMEM((KEYS, 128), BF16),
            pltpu.VMEM((KEYS, 256), BF16),
            pltpu.VMEM((4, 2, HALF, 128), BF16),
            pltpu.VMEM((4, 2, HALF, 128), BF16),
            pltpu.VMEM((4, 2, HALF, 128), BF16),
            pltpu.VMEM((4, 2, 8, 128), F32),
            pltpu.VMEM((4, 2, 8, 128), F32),
            pltpu.VMEM((4, HALF, 128), F32),
            pltpu.VMEM((4, HALF, 256), F32),
            dma((8, 3)), dma((5,)),
            dma((21,)), dma((21,)),
            dma((8,)), dma((8,)),
            dma((6,)), dma((6,)),
            dma((4,)), dma((4,)),
            dma((4, 2)), dma((4, 2)),
            dma((4, 2)), dma((4, 2)),
            dma((4, 2)), dma((4, 2)),
            dma((4, 2)), dma((4, 2)),
        ],
        compiler_params=pltpu.CompilerParams(
            collective_id=0, has_side_effects=True, vmem_limit_bytes=60 * 2**20
        ),
        name="star_query",
    )(
        hidden, norm_gain.reshape(64, 128), w_query, w_key, w_value,
        cache_keys, cache_values, cache_lengths, tables,
    )


def solution(mesh):
    placed = (
        P("ctx", "tensor"),
        P(),
        P(None, "tensor"),
        P(None, "tensor"),
        P(None, "tensor"),
        P("ctx", "tensor"),
        P("ctx", "tensor"),
        P("ctx"),
    )
    return jax.shard_map(
        local, mesh=mesh, in_specs=placed, out_specs=P("ctx", "tensor"), check_vma=False
    )
```
